512 devices in a mesh: ka: 16 (over z_lo, core), tau: 32 (over y, z_hi, x).
Axes of the slice: x: 4, y: 4, z: 16 (z_hi: 2, z_lo: 8; z = z_hi * 8 + z_lo), core: 2. Of those that a mesh axis runs over, the one named last changes fastest.
Arguments:
- bcoef: bfloat16 [16, 16, 384, 384], P('ka', None, 'tau'), may hold values from -0.3125 to 0.3125
- fwd_green: bfloat16 [16, 32, 384, 384], P('ka', 'tau'), may hold values from -0.3125 to 0.3125
- back_green: bfloat16 [16, 32, 384, 384], P('ka', 'tau'), may hold values from -0.3125 to 0.3125
- kmq: int32 [16], P('ka'), may hold values from 0 to 15, as said below
- ir_table: float32 [2, 128, 32], replicated, may hold values from -6 to 6
- ir_fit: float32 [32, 32], replicated, may hold values from -1 to 1
- freq_index: int32 [32], replicated, may hold values from 0 to 127
Outputs:
- polar_freq: float32 [2, 32, 16, 16], P(None, 'tau', 'ka')
The draws below stay inside these ranges and needn't reach their ends.
Inputs may be any that keep to these rules, and one draw needn't show every extreme that they name: kmq[k] is the index of k - q on a 4 x 4 grid of k-points numbered row by row with wrap-around, for one q whose two components are both nonzero (each 1 to 3); it is a permutation.
All inputs are finite; a program needn't handle non-finite values.
Results may differ from the reference program's by a relative error of at most 0.004.
Values may be sent and summed in bfloat16 or wider, within the bound.
No kernel may reach another device: no remote copies, remote signals or barrier semaphores. Data moves between devices by JAX's collectives and lax.ppermute only.
A program may use at most 64 MiB of HBM per device.

```python
import jax
import jax.numpy as jnp
from jax import lax

ORB = 384
NB = 16
K = 16
TAU = 32
NW = 32
NCAND = 128


def draw_kmq(key, part):
    key_major = jax.random.fold_in(key, 21)
    key_minor = jax.random.fold_in(key, 22)
    minor_size = K // 4
    shift_major = jax.random.randint(key_major, (), 1, 4)
    if minor_size > 1:
        shift_minor = jax.random.randint(key_minor, (), 1, minor_size)
    else:
        shift_minor = jnp.zeros((), jnp.int32)
    points = jnp.arange(K, dtype=jnp.int32)
    major_pos = points // minor_size
    minor_pos = points % minor_size
    mapped = (major_pos - shift_major) % 4 * minor_size + (minor_pos - shift_minor) % minor_size
    return mapped.astype(jnp.int32)


def plant(array, key, smallest, high):
    shape = array.shape
    place = [jax.random.randint(jax.random.fold_in(key, axis), (), 0, shape[axis]) for axis in range(len(shape))]
    array = array.at[tuple(place)].set(smallest)
    longest = shape.index(max(shape))
    place[longest] = (place[longest] + 1) % shape[longest]
    return array.at[tuple(place)].set(high)


def steps_of(key, extent, pieces, low, top_value):
    def one(axis_at, shards_of):
        heights = jax.random.uniform(jax.random.fold_in(jax.random.fold_in(key, 6), axis_at), (shards_of,), jnp.float32, low / len(pieces), top_value / len(pieces))
        return jnp.repeat(jnp.exp(heights), extent[axis_at] // shards_of).reshape((-1,) + (1,) * (len(extent) - axis_at - 1))

    loudness = one(*pieces[0])
    for cut in pieces[1:]:
        loudness = loudness * one(*cut)
    return loudness


def noise(rng, shape, scale, bound, pieces=(), held_as=jnp.bfloat16):
    array = scale * jax.random.normal(rng, shape, jnp.float32)
    if pieces:
        array = array * steps_of(rng, shape, pieces, -0.22, 0.18)
    return jnp.clip(array, -bound, bound).astype(held_as)


def setup_inputs(seed: int = 0) -> dict:
    arg_keys = jax.random.split(jax.random.key(seed), 8)
    return {
        "bcoef": noise(arg_keys[0], (K, NB, ORB, ORB), ORB ** -0.5, 0.3125, ((0, 16), (2, 32))),
        "fwd_green": noise(arg_keys[1], (K, TAU, ORB, ORB), ORB ** -0.5, 0.3125, ((0, 16), (1, 32))),
        "back_green": noise(arg_keys[2], (K, TAU, ORB, ORB), ORB ** -0.5, 0.3125, ((0, 16), (1, 32))),
        "kmq": draw_kmq(jax.random.fold_in(arg_keys[7], 71), 0),
        "ir_table": noise(arg_keys[4], (2, NCAND, TAU), 1.0, 6.0, (), jnp.float32),
        "ir_fit": noise(arg_keys[5], (TAU, TAU), TAU ** -0.5, 1.0, (), jnp.float32),
        "freq_index": plant(jax.random.randint(arg_keys[6], (NW,), 0, NCAND), jax.random.fold_in(arg_keys[6], 1), 0, NCAND - 1).astype(jnp.int32),
    }


def pair_term(coef_k, green_fwd, green_back):
    coef_wide = coef_k.astype(jnp.float32)
    left = jnp.einsum('pij,jl->pil', coef_wide, green_fwd.astype(jnp.float32)).astype(jnp.bfloat16)
    right = jnp.einsum('mi,qml->qil', green_back.astype(jnp.float32), coef_wide).astype(jnp.bfloat16)
    blocks = left.shape[0]
    return jnp.dot(left.reshape(blocks, -1), right.reshape(blocks, -1).T, preferred_element_type=jnp.float32)


def reference(bcoef, fwd_green, back_green, kmq, ir_table, ir_fit, freq_index):
    def one_time(time_step):
        def add_point(k_point, totals):
            partner = kmq[k_point]
            return totals + pair_term(bcoef[k_point], fwd_green[k_point, time_step], back_green[partner, time_step])

        summed = lax.fori_loop(0, K, add_point, jnp.zeros((NB, NB), jnp.float32))
        return summed * (-1.0 / K)

    polar_time = lax.map(one_time, jnp.arange(TAU))
    chosen = ir_table[:, freq_index, :]
    transform = jnp.einsum('cwl,lt->cwt', chosen, ir_fit, precision=lax.Precision.HIGHEST)
    return jnp.einsum('cwt,tpq->cwpq', transform, polar_time, precision=lax.Precision.HIGHEST)
```

```python
import functools

import jax
import jax.numpy as jnp
from jax import lax
from jax.experimental import pallas as pl
from jax.experimental.pallas import tpu as pltpu
from jax.sharding import Mesh
from jax.sharding import PartitionSpec as P

SIDE = 4
BLOCK = 16


def contract_kernel(b_ref, fwd_ref, back_t_ref, out_ref, left_ref, right_ref):
    blocks = b_ref.shape[0]
    orb = b_ref.shape[1]

    @pl.loop(0, blocks)
    def _(p):
        coef = b_ref[p]
        left = jnp.dot(coef, fwd_ref[...], preferred_element_type=jnp.float32)
        left_ref[p] = left.astype(jnp.bfloat16)
        right = jnp.dot(back_t_ref[...], coef, preferred_element_type=jnp.float32)
        right_ref[p] = right.astype(jnp.bfloat16)

    rows = blocks * BLOCK
    gram = jnp.zeros((rows, rows), jnp.float32)
    for at in range(0, orb, BLOCK):
        left = left_ref[:, at : at + BLOCK, :].reshape(rows, orb)
        right = right_ref[:, at : at + BLOCK, :].reshape(rows, orb)
        gram += lax.dot_general(
            left, right, (((1,), (1,)), ((), ())), preferred_element_type=jnp.float32
        )
    out_ref[...] = gram


def contract(coef, green_fwd, green_back_t):
    blocks, orb, _ = coef.shape
    rows = blocks * BLOCK
    gram = pl.pallas_call(
        contract_kernel,
        out_shape=jax.ShapeDtypeStruct((rows, rows), jnp.float32),
        in_specs=[pl.BlockSpec(memory_space=pltpu.VMEM)] * 3,
        out_specs=pl.BlockSpec(memory_space=pltpu.VMEM),
        scratch_shapes=[
            pltpu.VMEM((blocks, orb, orb), jnp.bfloat16),
            pltpu.VMEM((blocks, orb, orb), jnp.bfloat16),
        ],
        compiler_params=pltpu.CompilerParams(vmem_limit_bytes=40 * 1024 * 1024),
    )(coef, green_fwd, green_back_t)
    gram = gram.reshape(blocks, BLOCK, blocks, BLOCK)
    same = jnp.eye(BLOCK, dtype=jnp.float32)[None, :, None, :]
    return jnp.sum(gram * same, axis=(1, 3))


def spread(block, axes, count):
    copies = jnp.broadcast_to(block[None], (count,) + block.shape)
    return lax.all_to_all(copies, axes, 0, 0, tiled=True)


def shards(sizes, bcoef, fwd_green, back_green, kmq, ir_table, ir_fit, freq_index):
    zl, cores, ys, zh, xs = (sizes[name] for name in ("zl", "c", "y", "zh", "x"))
    blocks, rows, orb = bcoef.shape[1:]
    points = zl * cores
    minor = points // SIDE
    core = lax.axis_index("c")
    high = lax.axis_index("zh")
    low = lax.axis_index("zl")
    here_y, here_x = lax.axis_index("y"), lax.axis_index("x")

    own_k = low * cores + core
    target = kmq[0]
    major_shift = (own_k // minor - target // minor) % SIDE
    minor_shift = (own_k % minor - target % minor) % minor
    branch = (major_shift - 1) * (minor - 1) + minor_shift - 1

    transposed = [(c * zh + h, h * zh + c) for c in range(cores) for h in range(zh)]
    shard = lax.ppermute(bcoef.reshape(blocks * rows, orb), ("c", "zh"), transposed)
    green_fwd = lax.ppermute(fwd_green[0, 0], ("c", "zh"), transposed)

    def partner(major, minor_by):
        route = []
        for k in range(points):
            a, b = divmod(k, minor)
            source = (a - major) % SIDE * minor + (b - minor_by) % minor
            for h in range(zh):
                give = (source // cores * cores + source % cores) * zh + h
                take = (k // cores * cores + h) * zh + k % cores
                route.append((give, take))

        def move(block):
            return lax.ppermute(block, ("zl", "c", "zh"), route)

        return move

    moves = [partner(a, b) for a in range(1, SIDE) for b in range(1, minor)]
    green_back = lax.switch(branch, moves, back_green[0, 0])

    mine = spread(shard, ("y", "x"), ys * xs)
    other = lax.ppermute(mine, "c", [(0, 1), (1, 0)])
    first = jnp.where(core == 0, mine, other)
    second = jnp.where(core == 0, other, mine)
    both = jnp.stack([first, second]).reshape(cores, ys, xs, blocks, rows, orb)
    coef = both.transpose(3, 1, 0, 2, 4, 5).reshape(blocks, orb, orb)

    polar = contract(coef, green_fwd, green_back.T) * (-1.0 / points)

    pairs = polar.reshape(zl, 1, cores, blocks)
    pairs = jnp.broadcast_to(pairs, (zl, zh, cores, blocks)).reshape(zl * zh, cores, blocks)
    parts = lax.all_to_all(pairs, ("zl", "zh"), 0, 0, tiled=True)
    summed = jnp.sum(parts, axis=0)
    entries = jnp.broadcast_to(summed[:, None, :], (cores, ys * xs, blocks))
    entries = entries.reshape(cores * ys * xs, blocks)
    times = lax.all_to_all(entries, ("c", "y", "x"), 0, 0, tiled=True)

    own_w = (here_y * zh + high) * xs + here_x
    chosen = lax.dynamic_slice_in_dim(ir_table, freq_index[own_w], 1, axis=1)
    fit = ir_fit.reshape(-1, ys, cores, xs).transpose(0, 2, 1, 3).reshape(ir_fit.shape)
    transform = jnp.sum(chosen.transpose(0, 2, 1) * fit[None], axis=1)
    result = jnp.sum(transform[:, :, None] * times[None], axis=1)
    return result[:, None, None, :]


def solution(mesh):
    sizes = {"zl": 8, "c": 2, "y": 4, "zh": 2, "x": 4}
    fine = Mesh(mesh.devices.reshape(tuple(sizes.values())), tuple(sizes))
    ka, tau = ("zl", "c"), ("y", "zh", "x")
    return jax.shard_map(
        functools.partial(shards, sizes),
        mesh=fine,
        in_specs=(
            P(ka, None, tau, None),
            P(ka, tau, None, None),
            P(ka, tau, None, None),
            P(ka),
            P(),
            P(),
            P(),
        ),
        out_specs=P(None, tau, ka, None),
        check_vma=False,
    )
```

```python
import functools

import jax
import jax.numpy as jnp
from jax import lax
from jax.experimental import pallas as pl
from jax.experimental.pallas import tpu as pltpu
from jax.sharding import Mesh
from jax.sharding import PartitionSpec as P

SIDE = 4
TILE = 16
VMEM_LIMIT = 24 * 1024 * 1024


def onehot(rows, columns):
    return (rows == columns).astype(jnp.float32).astype(jnp.bfloat16)


def swap_order(blocks):
    size = TILE * blocks
    at = lax.broadcasted_iota(jnp.int32, (size, size), 0)
    source = lax.broadcasted_iota(jnp.int32, (size, size), 1)
    return onehot(at % TILE * blocks + at // TILE, source)


def ordered(order, piece_ref, group, blocks):
    size = TILE * blocks
    piece = piece_ref[pl.ds(pl.multiple_of(group * size, size), size), :]
    return jnp.dot(order, piece, preferred_element_type=jnp.float32).astype(jnp.bfloat16)


def left_kernel(mine_ref, fwd_ref, coef_ref, left_ref):
    blocks = coef_ref.shape[0]
    width = fwd_ref.shape[-1]
    order = swap_order(blocks)

    @pl.loop(0, coef_ref.shape[1] // TILE)
    def _(group):
        coef = ordered(order, mine_ref, group, blocks)
        left = jnp.dot(coef, fwd_ref[...], preferred_element_type=jnp.float32)
        spot = pl.ds(pl.multiple_of(group * TILE, TILE), TILE)
        coef_ref[:, spot, :] = coef.reshape(blocks, TILE, width)
        left_ref[:, spot, :] = left.astype(jnp.bfloat16).reshape(blocks, TILE, width)


def product_kernel(
    core_ref, coef_mine_ref, left_mine_ref, other_ref, fwd_ref, back_ref, out_ref, coef_ref, left_ref, back_t_ref, right_ref
):
    blocks, half, width = coef_mine_ref.shape
    core = core_ref[0]
    order = swap_order(blocks)
    run = 3 * TILE

    @pl.loop(0, half // TILE)
    def _(group):
        coef = ordered(order, other_ref, group, blocks)
        left = jnp.dot(coef, fwd_ref[...], preferred_element_type=jnp.float32)
        spot = pl.ds(pl.multiple_of(group * TILE, TILE), TILE)
        coef_ref[:, spot, :] = coef.reshape(blocks, TILE, width)
        left_ref[:, spot, :] = left.astype(jnp.bfloat16).reshape(blocks, TILE, width)

    def picked(side):
        starts = [pl.multiple_of(y * 2 * run + side * run, TILE) for y in range(SIDE)]
        return jnp.concatenate([back_ref[pl.ds(at, run), :] for at in starts], axis=0)

    back_t_ref[0] = picked(core).T
    back_t_ref[1] = picked(1 - core).T

    @pl.loop(0, blocks)
    def _(p):
        right = jnp.dot(back_t_ref[0], coef_mine_ref[p], preferred_element_type=jnp.float32)
        right += jnp.dot(back_t_ref[1], coef_ref[p], preferred_element_type=jnp.float32)
        right_ref[p] = right.astype(jnp.bfloat16)

    size = TILE * blocks
    gram = jnp.zeros((size, size), jnp.float32)
    for side, lefts in ((core, left_mine_ref), (1 - core, left_ref)):
        for y in range(SIDE):
            for part in range(run // TILE):
                at = y * run + part * TILE
                natural = pl.multiple_of(y * 2 * run + side * run + part * TILE, TILE)
                left = lefts[:, at : at + TILE, :].reshape(size, width)
                right = right_ref[:, pl.ds(natural, TILE), :].reshape(size, width)
                gram += lax.dot_general(
                    left, right, (((1,), (1,)), ((), ())), preferred_element_type=jnp.float32
                )
    row = lax.broadcasted_iota(jnp.int32, (size, size), 0) % TILE
    column = lax.broadcasted_iota(jnp.int32, (size, size), 1) % TILE
    gram = jnp.where(row == column, gram, 0.0)
    gram = jnp.sum(gram.reshape(blocks, TILE, size), axis=1)
    at = lax.broadcasted_iota(jnp.int32, (size, blocks), 0) // TILE
    which = lax.broadcasted_iota(jnp.int32, (size, blocks), 1)
    pick = (at == which).astype(jnp.float32)
    out_ref[...] = jnp.dot(
        gram, pick, precision=lax.Precision.HIGHEST, preferred_element_type=jnp.float32
    )


def left_half(mine, green_fwd, blocks):
    width = green_fwd.shape[-1]
    shape = jax.ShapeDtypeStruct((blocks, mine.shape[0] // blocks, width), jnp.bfloat16)
    return pl.pallas_call(
        left_kernel,
        out_shape=(shape, shape),
        in_specs=[pl.BlockSpec(memory_space=pltpu.VMEM)] * 2,
        out_specs=[pl.BlockSpec(memory_space=pltpu.VMEM)] * 2,
        compiler_params=pltpu.CompilerParams(vmem_limit_bytes=VMEM_LIMIT),
        cost_estimate=pl.CostEstimate(
            flops=2_000_000_000, bytes_accessed=7_000_000, transcendentals=0
        ),
    )(mine, green_fwd)


def product(core, coef_mine, left_mine, other, green_fwd, green_back):
    blocks, half, width = coef_mine.shape
    return pl.pallas_call(
        product_kernel,
        out_shape=jax.ShapeDtypeStruct((blocks, blocks), jnp.float32),
        in_specs=[pl.BlockSpec(memory_space=pltpu.SMEM)]
        + [pl.BlockSpec(memory_space=pltpu.VMEM)] * 5,
        out_specs=pl.BlockSpec(memory_space=pltpu.VMEM),
        scratch_shapes=[
            pltpu.VMEM((blocks, half, width), jnp.bfloat16),
            pltpu.VMEM((blocks, half, width), jnp.bfloat16),
            pltpu.VMEM((2, width, half), jnp.bfloat16),
            pltpu.VMEM((blocks, width, width), jnp.bfloat16),
        ],
        compiler_params=pltpu.CompilerParams(vmem_limit_bytes=VMEM_LIMIT),
        cost_estimate=pl.CostEstimate(
            flops=5_000_000_000, bytes_accessed=10_000_000, transcendentals=0
        ),
    )(core, coef_mine, left_mine, other, green_fwd, green_back)


def spread(block, axes, count):
    copies = jnp.broadcast_to(block[None], (count,) + block.shape)
    return lax.all_to_all(copies, axes, 0, 0, tiled=True)


def shards(sizes, bcoef, fwd_green, back_green, kmq, ir_table, ir_fit, freq_index):
    zl, cores, ys, zh, xs = (sizes[name] for name in ("zl", "c", "y", "zh", "x"))
    blocks, rows, orb = bcoef.shape[1:]
    points = zl * cores
    minor = points // SIDE
    core = lax.axis_index("c")
    high = lax.axis_index("zh")
    low = lax.axis_index("zl")
    here_y, here_x = lax.axis_index("y"), lax.axis_index("x")

    own_k = low * cores + core
    target = kmq[0]
    major_shift = ((own_k >> 2) - (target >> 2)) & 3
    minor_shift = ((own_k & 3) - (target & 3)) & 3
    branch = (major_shift - 1) * (minor - 1) + minor_shift - 1

    transposed = [(c * zh + h, h * zh + c) for c in range(cores) for h in range(zh)]

    def partner(major, minor_by):
        route = []
        for k in range(points):
            a, b = divmod(k, minor)
            source = (a - major) % SIDE * minor + (b - minor_by) % minor
            for h in range(zh):
                route.append((source * zh + h, (k // cores * cores + h) * zh + k % cores))

        def work(shard, green_fwd, green_back):
            shard = shard.transpose(1, 0, 2).reshape(rows * blocks, orb)
            shard = lax.ppermute(shard, ("c", "zh"), transposed)
            green_fwd = lax.ppermute(green_fwd, ("c", "zh"), transposed)
            green_back = lax.ppermute(green_back, ("zl", "c", "zh"), route)
            mine = spread(shard, ("y", "x"), ys * xs).reshape(ys * xs * rows * blocks, orb)
            mine, green_fwd, green_back = lax.optimization_barrier((mine, green_fwd, green_back))
            other = lax.ppermute(mine, "c", [(0, 1), (1, 0)])
            coef_mine, left_mine = left_half(mine, green_fwd, blocks)
            return product(core[None], coef_mine, left_mine, other, green_fwd, green_back)

        return work

    works = [partner(a, b) for a in range(1, SIDE) for b in range(1, minor)]
    polar = lax.switch(branch, works, bcoef[0], fwd_green[0, 0], back_green[0, 0])
    polar = polar * (-1.0 / points)

    pairs = polar.reshape(zl, 1, cores, blocks)
    pairs = jnp.broadcast_to(pairs, (zl, zh, cores, blocks)).reshape(zl * zh, cores, blocks)
    parts = lax.all_to_all(pairs, ("zl", "zh"), 0, 0, tiled=True)
    summed = jnp.sum(parts, axis=0)
    entries = jnp.broadcast_to(summed[:, None, :], (cores, ys * xs, blocks))
    entries = entries.reshape(cores * ys * xs, blocks)
    times = lax.all_to_all(entries, ("c", "y", "x"), 0, 0, tiled=True)

    own_w = (here_y * zh + high) * xs + here_x
    chosen = lax.dynamic_slice_in_dim(ir_table, freq_index[own_w], 1, axis=1)
    fit = ir_fit.reshape(-1, ys, cores, xs).transpose(0, 2, 1, 3).reshape(ir_fit.shape)
    transform = jnp.sum(chosen.transpose(0, 2, 1) * fit[None], axis=1)
    result = jnp.sum(transform[:, :, None] * times[None], axis=1)
    return result[:, None, None, :]


def solution(mesh):
    sizes = {"zl": 8, "c": 2, "y": 4, "zh": 2, "x": 4}
    fine = Mesh(mesh.devices.reshape(tuple(sizes.values())), tuple(sizes))
    ka, tau = ("zl", "c"), ("y", "zh", "x")
    return jax.shard_map(
        functools.partial(shards, sizes),
        mesh=fine,
        in_specs=(
            P(ka, None, tau, None),
            P(ka, tau, None, None),
            P(ka, tau, None, None),
            P(ka),
            P(),
            P(),
            P(),
        ),
        out_specs=P(None, tau, ka, None),
        check_vma=False,
    )
```

```python
import functools

import jax
import jax.numpy as jnp
from jax import lax
from jax.experimental import pallas as pl
from jax.experimental.pallas import tpu as pltpu
from jax.sharding import Mesh
from jax.sharding import PartitionSpec as P

SIDE = 4
TILE = 16
POINTS = 16
VMEM_LIMIT = 24 * 1024 * 1024
COST = pl.CostEstimate(flops=1000, bytes_accessed=1000, transcendentals=0)


def onehot(rows, columns):
    return (rows == columns).astype(jnp.float32).astype(jnp.bfloat16)


def swap_order(blocks):
    size = TILE * blocks
    at = lax.broadcasted_iota(jnp.int32, (size, size), 0)
    source = lax.broadcasted_iota(jnp.int32, (size, size), 1)
    return onehot(at % TILE * blocks + at // TILE, source)


def ordered(order, piece_ref, group, blocks):
    size = TILE * blocks
    piece = piece_ref[pl.ds(pl.multiple_of(group * size, size), size), :]
    return jnp.dot(order, piece, preferred_element_type=jnp.float32).astype(jnp.bfloat16)


def left_kernel(piece_ref, fwd_ref, coef_ref, left_ref):
    blocks = coef_ref.shape[0]
    width = fwd_ref.shape[-1]
    order = swap_order(blocks)
    step = 3

    @pl.loop(0, coef_ref.shape[1] // TILE // step)
    def _(turn):
        coefs = []
        for part in range(step):
            group = turn * step + part
            coef = ordered(order, piece_ref, group, blocks)
            spot = pl.ds(pl.multiple_of(group * TILE, TILE), TILE)
            coef_ref[:, spot, :] = coef.reshape(blocks, TILE, width)
            coefs.append(coef)
        left = jnp.dot(
            jnp.concatenate(coefs, axis=0), fwd_ref[...], preferred_element_type=jnp.float32
        )
        left = left.astype(jnp.bfloat16).reshape(step, blocks, TILE, width)
        for part in range(step):
            group = turn * step + part
            spot = pl.ds(pl.multiple_of(group * TILE, TILE), TILE)
            left_ref[:, spot, :] = left[part]


def product_kernel(
    core_ref, coef_mine_ref, coef_other_ref, left_mine_ref, left_other_ref, upper_ref, lower_ref, out_ref, back_t_ref, right_ref
):
    blocks, half, width = coef_mine_ref.shape
    core = core_ref[0]
    run = 3 * TILE

    def picked(side):
        starts = [pl.multiple_of(y * 2 * run + side * run, TILE) for y in range(SIDE // 2)]
        refs = (upper_ref, lower_ref)
        return jnp.concatenate([ref[pl.ds(at, run), :] for ref in refs for at in starts], axis=0)

    back_t_ref[...] = jnp.concatenate([picked(core), picked(1 - core)], axis=0).T

    @pl.loop(0, blocks // 2)
    def _(pair):
        coefs = []
        for p in (2 * pair, 2 * pair + 1):
            coefs.append(jnp.concatenate([coef_mine_ref[p], coef_other_ref[p]], axis=0))
        right = jnp.dot(
            back_t_ref[...], jnp.concatenate(coefs, axis=1), preferred_element_type=jnp.float32
        )
        right = right.astype(jnp.bfloat16)
        right_ref[2 * pair] = right[:, :width]
        right_ref[2 * pair + 1] = right[:, width:]

    size = TILE * blocks
    gram = jnp.zeros((size, size), jnp.float32)
    for side, lefts in ((core, left_mine_ref), (1 - core, left_other_ref)):
        for y in range(SIDE):
            left_parts, right_parts = [], []
            for part in range(run // TILE):
                at = y * run + part * TILE
                natural = pl.multiple_of(y * 2 * run + side * run + part * TILE, TILE)
                left_parts.append(lefts[:, at : at + TILE, :].reshape(size, width))
                right_parts.append(right_ref[:, pl.ds(natural, TILE), :].reshape(size, width))
            gram += lax.dot_general(
                jnp.concatenate(left_parts, axis=1),
                jnp.concatenate(right_parts, axis=1),
                (((1,), (1,)), ((), ())),
                preferred_element_type=jnp.float32,
            )
    row = lax.broadcasted_iota(jnp.int32, (size, size), 0) % TILE
    column = lax.broadcasted_iota(jnp.int32, (size, size), 1) % TILE
    gram = jnp.where(row == column, gram, 0.0)
    gram = jnp.sum(gram.reshape(blocks, TILE, size), axis=1)
    at = lax.broadcasted_iota(jnp.int32, (size, blocks), 0) // TILE
    which = lax.broadcasted_iota(jnp.int32, (size, blocks), 1)
    pick = (at == which).astype(jnp.float32)
    polar = jnp.dot(gram, pick, precision=lax.Precision.HIGHEST, preferred_element_type=jnp.float32)
    out_ref[...] = polar * (-1.0 / POINTS)


def left_half(piece, green_fwd, blocks):
    width = green_fwd.shape[-1]
    shape = jax.ShapeDtypeStruct((blocks, piece.shape[0] // blocks, width), jnp.bfloat16)
    return pl.pallas_call(
        left_kernel,
        out_shape=(shape, shape),
        in_specs=[pl.BlockSpec(memory_space=pltpu.VMEM)] * 2,
        out_specs=[pl.BlockSpec(memory_space=pltpu.VMEM)] * 2,
        compiler_params=pltpu.CompilerParams(vmem_limit_bytes=VMEM_LIMIT),
        cost_estimate=COST,
    )(piece, green_fwd)


def product(core, coef_mine, coef_other, left_mine, left_other, upper, lower):
    blocks, half, width = coef_mine.shape
    return pl.pallas_call(
        product_kernel,
        out_shape=jax.ShapeDtypeStruct((blocks, blocks), jnp.float32),
        in_specs=[pl.BlockSpec(memory_space=pltpu.SMEM)]
        + [pl.BlockSpec(memory_space=pltpu.VMEM)] * 6,
        out_specs=pl.BlockSpec(memory_space=pltpu.VMEM),
        scratch_shapes=[
            pltpu.VMEM((width, width), jnp.bfloat16),
            pltpu.VMEM((blocks, width, width), jnp.bfloat16),
        ],
        compiler_params=pltpu.CompilerParams(vmem_limit_bytes=VMEM_LIMIT),
        cost_estimate=COST,
    )(core, coef_mine, coef_other, left_mine, left_other, upper, lower)


def spread(block, axes, count):
    copies = jnp.broadcast_to(block[None], (count,) + block.shape)
    return lax.all_to_all(copies, axes, 0, 0, tiled=True)


def shards(sizes, bcoef, fwd_green, back_green, kmq, ir_table, ir_fit, freq_index):
    zl, cores, ys, zh, xs = (sizes[name] for name in ("zl", "c", "y", "zh", "x"))
    blocks, rows, orb = bcoef.shape[1:]
    points = zl * cores
    minor = points // SIDE
    core = lax.axis_index("c")
    high = lax.axis_index("zh")
    low = lax.axis_index("zl")
    here_y, here_x = lax.axis_index("y"), lax.axis_index("x")

    own_k = low * cores + core
    target = kmq[0]
    major_shift = ((own_k >> 2) - (target >> 2)) & 3
    minor_shift = ((own_k & 3) - (target & 3)) & 3
    branch = (major_shift - 1) * (minor - 1) + minor_shift - 1

    transposed = [(c * zh + h, h * zh + c) for c in range(cores) for h in range(zh)]

    def partner(major, minor_by):
        route = []
        for k in range(points):
            a, b = divmod(k, minor)
            source = (a - major) % SIDE * minor + (b - minor_by) % minor
            for h in range(zh):
                route.append((source * zh + h, (k // cores * cores + h) * zh + k % cores))

        def work(shard, green_fwd, green_back):
            shard = shard.transpose(1, 0, 2).reshape(rows * blocks, orb)
            shard = lax.ppermute(shard, ("c", "zh"), transposed)
            green_fwd = lax.ppermute(green_fwd, ("c", "zh"), transposed)
            upper, lower = green_back[: orb // 2], green_back[orb // 2 :]
            upper = lax.ppermute(upper, ("zl", "c", "zh"), route)
            lower = lax.ppermute(lower, ("zl", "c", "zh"), route)
            mine = lax.cond(
                target >= 0,
                lambda block: spread(block, ("y", "x"), ys * xs),
                lambda block: jnp.zeros((ys * xs,) + block.shape, block.dtype),
                shard,
            )
            mine = mine.reshape(ys * xs * rows * blocks, orb)
            mine, green_fwd, upper = lax.optimization_barrier((mine, green_fwd, upper))
            other = lax.ppermute(mine, "c", [(0, 1), (1, 0)])
            coef_mine, left_mine = left_half(mine, green_fwd, blocks)
            coef_other, left_other = left_half(other, green_fwd, blocks)
            return product(core[None], coef_mine, coef_other, left_mine, left_other, upper, lower)

        return work

    works = [partner(a, b) for a in range(1, SIDE) for b in range(1, minor)]
    polar = lax.switch(branch, works, bcoef[0], fwd_green[0, 0], back_green[0, 0])

    pairs = polar.reshape(zl, 1, cores, blocks)
    pairs = jnp.broadcast_to(pairs, (zl, zh, cores, blocks)).reshape(zl * zh, cores, blocks)
    parts = lax.all_to_all(pairs, ("zl", "zh"), 0, 0, tiled=True)
    summed = jnp.sum(parts, axis=0)
    entries = jnp.broadcast_to(summed[:, None, :], (cores, ys * xs, blocks))
    entries = entries.reshape(cores * ys * xs, blocks)
    times = lax.all_to_all(entries, ("c", "y", "x"), 0, 0, tiled=True)

    own_w = (here_y * zh + high) * xs + here_x
    chosen = lax.dynamic_slice_in_dim(ir_table, freq_index[own_w], 1, axis=1)
    fit = ir_fit.reshape(-1, ys, cores, xs).transpose(0, 2, 1, 3).reshape(ir_fit.shape)
    transform = jnp.sum(chosen.transpose(0, 2, 1) * fit[None], axis=1)
    result = jnp.sum(transform[:, :, None] * times[None], axis=1)
    return result[:, None, None, :]


def solution(mesh):
    sizes = {"zl": 8, "c": 2, "y": 4, "zh": 2, "x": 4}
    fine = Mesh(mesh.devices.reshape(tuple(sizes.values())), tuple(sizes))
    ka, tau = ("zl", "c"), ("y", "zh", "x")
    return jax.shard_map(
        functools.partial(shards, sizes),
        mesh=fine,
        in_specs=(
            P(ka, None, tau, None),
            P(ka, tau, None, None),
            P(ka, tau, None, None),
            P(ka),
            P(),
            P(),
            P(),
        ),
        out_specs=P(None, tau, ka, None),
        check_vma=False,
    )
```

```python
import functools

import jax
import jax.numpy as jnp
from jax import lax
from jax.experimental import pallas as pl
from jax.experimental.pallas import tpu as pltpu
from jax.sharding import Mesh
from jax.sharding import PartitionSpec as P

SIDE = 4
TILE = 16
POINTS = 16
VMEM_LIMIT = 24 * 1024 * 1024
SMALL_LIMIT = 8 * 1024 * 1024
COST = pl.CostEstimate(flops=1000, bytes_accessed=1000, transcendentals=0)


def onehot(rows, columns):
    return (rows == columns).astype(jnp.float32).astype(jnp.bfloat16)


def swap_order(blocks):
    size = TILE * blocks
    at = lax.broadcasted_iota(jnp.int32, (size, size), 0)
    source = lax.broadcasted_iota(jnp.int32, (size, size), 1)
    return onehot(at % TILE * blocks + at // TILE, source)


def ordered(order, piece_ref, group, blocks):
    size = TILE * blocks
    piece = piece_ref[pl.ds(pl.multiple_of(group * size, size), size), :]
    return jnp.dot(order, piece, preferred_element_type=jnp.float32).astype(jnp.bfloat16)


def left_kernel(piece_ref, fwd_ref, coef_ref, left_ref):
    blocks = coef_ref.shape[0]
    width = fwd_ref.shape[-1]
    order = swap_order(blocks)
    step = 3

    @pl.loop(0, coef_ref.shape[1] // TILE // step)
    def _(turn):
        coefs = []
        for part in range(step):
            group = turn * step + part
            coef = ordered(order, piece_ref, group, blocks)
            spot = pl.ds(pl.multiple_of(group * TILE, TILE), TILE)
            coef_ref[:, spot, :] = coef.reshape(blocks, TILE, width)
            coefs.append(coef)
        left = jnp.dot(
            jnp.concatenate(coefs, axis=0), fwd_ref[...], preferred_element_type=jnp.float32
        )
        left = left.astype(jnp.bfloat16).reshape(step, blocks, TILE, width)
        for part in range(step):
            group = turn * step + part
            spot = pl.ds(pl.multiple_of(group * TILE, TILE), TILE)
            left_ref[:, spot, :] = left[part]


def turn_kernel(side_ref, back_ref, out_ref):
    side = side_ref[0]
    run = 3 * TILE

    def picked(side):
        starts = [pl.multiple_of(y * 2 * run + side * run, TILE) for y in range(SIDE)]
        return jnp.concatenate([back_ref[pl.ds(at, run), :] for at in starts], axis=0)

    out_ref[...] = jnp.concatenate([picked(side), picked(1 - side)], axis=0).T


def turned(side, green_back):
    return pl.pallas_call(
        turn_kernel,
        out_shape=jax.ShapeDtypeStruct(green_back.shape, green_back.dtype),
        in_specs=[
            pl.BlockSpec(memory_space=pltpu.SMEM),
            pl.BlockSpec(memory_space=pltpu.VMEM),
        ],
        out_specs=pl.BlockSpec(memory_space=pltpu.VMEM),
        compiler_params=pltpu.CompilerParams(vmem_limit_bytes=SMALL_LIMIT),
        cost_estimate=COST,
    )(side, green_back)


def product_kernel(
    core_ref, coef_mine_ref, coef_other_ref, left_mine_ref, left_other_ref, back_t_ref, out_ref, right_ref
):
    blocks, half, width = coef_mine_ref.shape
    core = core_ref[0]
    run = 3 * TILE

    @pl.loop(0, blocks // 2)
    def _(pair):
        coefs = []
        for p in (2 * pair, 2 * pair + 1):
            coefs.append(jnp.concatenate([coef_mine_ref[p], coef_other_ref[p]], axis=0))
        right = jnp.dot(
            back_t_ref[...], jnp.concatenate(coefs, axis=1), preferred_element_type=jnp.float32
        )
        right = right.astype(jnp.bfloat16)
        right_ref[2 * pair] = right[:, :width]
        right_ref[2 * pair + 1] = right[:, width:]

    size = TILE * blocks
    gram = jnp.zeros((size, size), jnp.float32)
    for side, lefts in ((core, left_mine_ref), (1 - core, left_other_ref)):
        for y in range(SIDE):
            left_parts, right_parts = [], []
            for part in range(run // TILE):
                at = y * run + part * TILE
                natural = pl.multiple_of(y * 2 * run + side * run + part * TILE, TILE)
                left_parts.append(lefts[:, at : at + TILE, :].reshape(size, width))
                right_parts.append(right_ref[:, pl.ds(natural, TILE), :].reshape(size, width))
            gram += lax.dot_general(
                jnp.concatenate(left_parts, axis=1),
                jnp.concatenate(right_parts, axis=1),
                (((1,), (1,)), ((), ())),
                preferred_element_type=jnp.float32,
            )
    row = lax.broadcasted_iota(jnp.int32, (size, size), 0) % TILE
    column = lax.broadcasted_iota(jnp.int32, (size, size), 1) % TILE
    gram = jnp.where(row == column, gram, 0.0)
    gram = jnp.sum(gram.reshape(blocks, TILE, size), axis=1)
    at = lax.broadcasted_iota(jnp.int32, (size, blocks), 0) // TILE
    which = lax.broadcasted_iota(jnp.int32, (size, blocks), 1)
    pick = (at == which).astype(jnp.float32)
    polar = jnp.dot(gram, pick, precision=lax.Precision.HIGHEST, preferred_element_type=jnp.float32)
    polar = polar * (-1.0 / POINTS)
    _, cores, _ = out_ref.shape
    for p in range(blocks):
        for copy in range(out_ref.shape[0] * cores // blocks):
            place = p // cores * (out_ref.shape[0] * cores // blocks) + copy
            out_ref[place, p % cores : p % cores + 1, :] = polar[p : p + 1, :]


def left_half(piece, green_fwd, blocks):
    width = green_fwd.shape[-1]
    shape = jax.ShapeDtypeStruct((blocks, piece.shape[0] // blocks, width), jnp.bfloat16)
    return pl.pallas_call(
        left_kernel,
        out_shape=(shape, shape),
        in_specs=[pl.BlockSpec(memory_space=pltpu.VMEM)] * 2,
        out_specs=[pl.BlockSpec(memory_space=pltpu.VMEM)] * 2,
        compiler_params=pltpu.CompilerParams(vmem_limit_bytes=VMEM_LIMIT),
        cost_estimate=COST,
    )(piece, green_fwd)


def product(core, coef_mine, coef_other, left_mine, left_other, green_back, receivers, cores):
    blocks, half, width = coef_mine.shape
    return pl.pallas_call(
        product_kernel,
        out_shape=jax.ShapeDtypeStruct((receivers, cores, blocks), jnp.float32),
        in_specs=[pl.BlockSpec(memory_space=pltpu.SMEM)]
        + [pl.BlockSpec(memory_space=pltpu.VMEM)] * 5,
        out_specs=pl.BlockSpec(memory_space=pltpu.VMEM),
        scratch_shapes=[
            pltpu.VMEM((blocks, width, width), jnp.bfloat16),
        ],
        compiler_params=pltpu.CompilerParams(vmem_limit_bytes=VMEM_LIMIT),
        cost_estimate=COST,
    )(core, coef_mine, coef_other, left_mine, left_other, green_back)


def settle_kernel(block_ref, out_ref):
    out_ref[...] = block_ref[...]


def settled(block):
    return pl.pallas_call(
        settle_kernel,
        out_shape=jax.ShapeDtypeStruct(block.shape, block.dtype),
        in_specs=[pl.BlockSpec(memory_space=pltpu.VMEM)],
        out_specs=pl.BlockSpec(memory_space=pltpu.VMEM),
        compiler_params=pltpu.CompilerParams(vmem_limit_bytes=SMALL_LIMIT),
        cost_estimate=pl.CostEstimate(
            flops=50_000_000_000, bytes_accessed=2_500_000, transcendentals=0
        ),
    )(block)


def spread(block, axes, count):
    copies = jnp.broadcast_to(block[None], (count,) + block.shape)
    return lax.all_to_all(copies, axes, 0, 0, tiled=True)


def shards(sizes, bcoef, fwd_green, back_green, kmq, ir_table, ir_fit, freq_index):
    zl, cores, ys, zh, xs = (sizes[name] for name in ("zl", "c", "y", "zh", "x"))
    blocks, rows, orb = bcoef.shape[1:]
    points = zl * cores
    minor = points // SIDE
    core = lax.axis_index("c")
    high = lax.axis_index("zh")
    low = lax.axis_index("zl")
    here_y, here_x = lax.axis_index("y"), lax.axis_index("x")

    own_w = (here_y * zh + high) * xs + here_x
    own_k = low * cores + core
    target = kmq[0]
    major_shift = ((own_k >> 2) - (target >> 2)) & 3
    minor_shift = ((own_k & 3) - (target & 3)) & 3
    branch = (major_shift - 1) * (minor - 1) + minor_shift - 1

    transposed = [(c * zh + h, h * zh + c) for c in range(cores) for h in range(zh)]

    def partner(major, minor_by):
        route = []
        for k in range(points):
            a, b = divmod(k, minor)
            source = (a - major) % SIDE * minor + (b - minor_by) % minor
            for h in range(zh):
                route.append((source * zh + h, (k // cores * cores + h) * zh + k % cores))

        def work(shard, green_fwd, green_back):
            shard = shard.transpose(1, 0, 2).reshape(rows * blocks, orb)
            shard = lax.ppermute(shard, ("c", "zh"), transposed)
            green_fwd = lax.ppermute(green_fwd, ("c", "zh"), transposed)
            green_back = lax.ppermute(turned(high[None], green_back), ("zl", "c", "zh"), route)
            mine = lax.cond(
                target >= 0,
                lambda block: spread(block, ("y", "x"), ys * xs),
                lambda block: jnp.zeros((ys * xs,) + block.shape, block.dtype),
                settled(shard),
            )
            mine = mine.reshape(ys * xs * rows * blocks, orb)
            mine, green_fwd, green_back = lax.optimization_barrier((mine, green_fwd, green_back))
            other = lax.ppermute(mine, "c", [(0, 1), (1, 0)])
            coef_mine, left_mine = left_half(mine, green_fwd, blocks)
            coef_other, left_other = left_half(other, green_fwd, blocks)
            return product(
                core[None], coef_mine, coef_other, left_mine, left_other, green_back, zl * zh, cores
            )

        return work

    works = [partner(a, b) for a in range(1, SIDE) for b in range(1, minor)]
    pairs = lax.switch(branch, works, bcoef[0], fwd_green[0, 0], back_green[0, 0])
    parts = lax.all_to_all(pairs, ("zl", "zh"), 0, 0, tiled=True)
    summed = jnp.sum(parts, axis=0)
    entries = jnp.broadcast_to(summed[:, None, :], (cores, ys * xs, blocks))
    entries = entries.reshape(cores * ys * xs, blocks)
    times = lax.all_to_all(entries, ("c", "y", "x"), 0, 0, tiled=True)
    chosen = lax.dynamic_slice_in_dim(ir_table, freq_index[own_w], 1, axis=1)
    fit = ir_fit.reshape(-1, ys, cores, xs).transpose(0, 2, 1, 3).reshape(ir_fit.shape)
    transform = jnp.sum(chosen.transpose(0, 2, 1) * fit[None], axis=1)
    result = jnp.sum(transform[:, :, None] * times[None], axis=1)
    return result[:, None, None, :]


def solution(mesh):
    sizes = {"zl": 8, "c": 2, "y": 4, "zh": 2, "x": 4}
    fine = Mesh(mesh.devices.reshape(tuple(sizes.values())), tuple(sizes))
    ka, tau = ("zl", "c"), ("y", "zh", "x")
    return jax.shard_map(
        functools.partial(shards, sizes),
        mesh=fine,
        in_specs=(
            P(ka, None, tau, None),
            P(ka, tau, None, None),
            P(ka, tau, None, None),
            P(ka),
            P(),
            P(),
            P(),
        ),
        out_specs=P(None, tau, ka, None),
        check_vma=False,
    )
```

```python
import functools

import jax
import jax.numpy as jnp
from jax import lax
from jax.experimental import pallas as pl
from jax.experimental.pallas import tpu as pltpu
from jax.sharding import Mesh
from jax.sharding import PartitionSpec as P

SIDE = 4
TILE = 16
POINTS = 16
VMEM_LIMIT = 24 * 1024 * 1024
SMALL_LIMIT = 8 * 1024 * 1024
COST = pl.CostEstimate(flops=1000, bytes_accessed=1000, transcendentals=0)


def onehot(rows, columns):
    return (rows == columns).astype(jnp.float32).astype(jnp.bfloat16)


def swap_order(blocks):
    size = TILE * blocks
    at = lax.broadcasted_iota(jnp.int32, (size, size), 0)
    source = lax.broadcasted_iota(jnp.int32, (size, size), 1)
    return onehot(at % TILE * blocks + at // TILE, source)


def ordered(order, piece_ref, group, blocks):
    size = TILE * blocks
    piece = piece_ref[pl.ds(pl.multiple_of(group * size, size), size), :]
    return jnp.dot(order, piece, preferred_element_type=jnp.float32).astype(jnp.bfloat16)


def left_kernel(piece_ref, fwd_ref, coef_ref, left_ref):
    blocks = coef_ref.shape[0]
    width = fwd_ref.shape[-1]
    order = swap_order(blocks)
    step = 3

    @pl.loop(0, coef_ref.shape[1] // TILE // step)
    def _(turn):
        coefs = []
        for part in range(step):
            group = turn * step + part
            coef = ordered(order, piece_ref, group, blocks)
            spot = pl.ds(pl.multiple_of(group * TILE, TILE), TILE)
            coef_ref[:, spot, :] = coef.reshape(blocks, TILE, width)
            coefs.append(coef)
        left = jnp.dot(
            jnp.concatenate(coefs, axis=0), fwd_ref[...], preferred_element_type=jnp.float32
        )
        left = left.astype(jnp.bfloat16).reshape(step, blocks, TILE, width)
        for part in range(step):
            group = turn * step + part
            spot = pl.ds(pl.multiple_of(group * TILE, TILE), TILE)
            left_ref[:, spot, :] = left[part]


def turn_kernel(side_ref, back_ref, out_ref):
    side = side_ref[0]
    run = 3 * TILE

    def picked(side):
        starts = [pl.multiple_of(y * 2 * run + side * run, TILE) for y in range(SIDE)]
        return jnp.concatenate([back_ref[pl.ds(at, run), :] for at in starts], axis=0)

    out_ref[...] = jnp.concatenate([picked(side), picked(1 - side)], axis=0).T


def turned(side, green_back):
    return pl.pallas_call(
        turn_kernel,
        out_shape=jax.ShapeDtypeStruct(green_back.shape, green_back.dtype),
        in_specs=[
            pl.BlockSpec(memory_space=pltpu.SMEM),
            pl.BlockSpec(memory_space=pltpu.VMEM),
        ],
        out_specs=pl.BlockSpec(memory_space=pltpu.VMEM),
        compiler_params=pltpu.CompilerParams(vmem_limit_bytes=SMALL_LIMIT),
        cost_estimate=COST,
    )(side, green_back)


def product_kernel(
    core_ref, coef_mine_ref, coef_other_ref, left_mine_ref, left_other_ref, back_t_ref, out_ref, right_ref
):
    blocks, half, width = coef_mine_ref.shape
    core = core_ref[0]
    run = 3 * TILE

    @pl.loop(0, blocks // 2)
    def _(pair):
        coefs = []
        for p in (2 * pair, 2 * pair + 1):
            coefs.append(jnp.concatenate([coef_mine_ref[p], coef_other_ref[p]], axis=0))
        right = jnp.dot(
            back_t_ref[...], jnp.concatenate(coefs, axis=1), preferred_element_type=jnp.float32
        )
        right = right.astype(jnp.bfloat16)
        right_ref[2 * pair] = right[:, :width]
        right_ref[2 * pair + 1] = right[:, width:]

    size = TILE * blocks
    gram = jnp.zeros((size, size), jnp.float32)
    for side, lefts in ((core, left_mine_ref), (1 - core, left_other_ref)):
        for y in range(SIDE):
            left_parts, right_parts = [], []
            for part in range(run // TILE):
                at = y * run + part * TILE
                natural = pl.multiple_of(y * 2 * run + side * run + part * TILE, TILE)
                left_parts.append(lefts[:, at : at + TILE, :].reshape(size, width))
                right_parts.append(right_ref[:, pl.ds(natural, TILE), :].reshape(size, width))
            gram += lax.dot_general(
                jnp.concatenate(left_parts, axis=1),
                jnp.concatenate(right_parts, axis=1),
                (((1,), (1,)), ((), ())),
                preferred_element_type=jnp.float32,
            )
    row = lax.broadcasted_iota(jnp.int32, (size, size), 0) % TILE
    column = lax.broadcasted_iota(jnp.int32, (size, size), 1) % TILE
    gram = jnp.where(row == column, gram, 0.0)
    gram = jnp.sum(gram.reshape(blocks, TILE, size), axis=1)
    at = lax.broadcasted_iota(jnp.int32, (size, blocks), 0) // TILE
    which = lax.broadcasted_iota(jnp.int32, (size, blocks), 1)
    pick = (at == which).astype(jnp.float32)
    polar = jnp.dot(gram, pick, precision=lax.Precision.HIGHEST, preferred_element_type=jnp.float32)
    polar = polar * (-1.0 / POINTS)
    _, cores, _ = out_ref.shape
    for p in range(blocks):
        for copy in range(out_ref.shape[0] * cores // blocks):
            place = p // cores * (out_ref.shape[0] * cores // blocks) + copy
            out_ref[place, p % cores : p % cores + 1, :] = polar[p : p + 1, :]


def left_half(piece, green_fwd, blocks):
    width = green_fwd.shape[-1]
    shape = jax.ShapeDtypeStruct((blocks, piece.shape[0] // blocks, width), jnp.bfloat16)
    return pl.pallas_call(
        left_kernel,
        out_shape=(shape, shape),
        in_specs=[pl.BlockSpec(memory_space=pltpu.VMEM)] * 2,
        out_specs=[pl.BlockSpec(memory_space=pltpu.VMEM)] * 2,
        compiler_params=pltpu.CompilerParams(vmem_limit_bytes=VMEM_LIMIT),
        cost_estimate=COST,
    )(piece, green_fwd)


def product(core, coef_mine, coef_other, left_mine, left_other, green_back, receivers, cores):
    blocks, half, width = coef_mine.shape
    return pl.pallas_call(
        product_kernel,
        out_shape=jax.ShapeDtypeStruct((receivers, cores, blocks), jnp.float32),
        in_specs=[pl.BlockSpec(memory_space=pltpu.SMEM)]
        + [pl.BlockSpec(memory_space=pltpu.VMEM)] * 5,
        out_specs=pl.BlockSpec(memory_space=pltpu.VMEM),
        scratch_shapes=[
            pltpu.VMEM((blocks, width, width), jnp.bfloat16),
        ],
        compiler_params=pltpu.CompilerParams(vmem_limit_bytes=VMEM_LIMIT),
        cost_estimate=COST,
    )(core, coef_mine, coef_other, left_mine, left_other, green_back)


def spread(block, axes, count):
    copies = jnp.broadcast_to(block[None], (count,) + block.shape)
    return lax.all_to_all(copies, axes, 0, 0, tiled=True)


def shards(sizes, bcoef, fwd_green, back_green, kmq, ir_table, ir_fit, freq_index):
    zl, cores, ys, zh, xs = (sizes[name] for name in ("zl", "c", "y", "zh", "x"))
    blocks, rows, orb = bcoef.shape[1:]
    points = zl * cores
    minor = points // SIDE
    core = lax.axis_index("c")
    high = lax.axis_index("zh")
    low = lax.axis_index("zl")
    here_y, here_x = lax.axis_index("y"), lax.axis_index("x")

    own_w = (here_y * zh + high) * xs + here_x
    own_k = low * cores + core
    target = kmq[0]
    major_shift = ((own_k >> 2) - (target >> 2)) & 3
    minor_shift = ((own_k & 3) - (target & 3)) & 3
    branch = (major_shift - 1) * (minor - 1) + minor_shift - 1

    transposed = [(c * zh + h, h * zh + c) for c in range(cores) for h in range(zh)]

    def partner(major, minor_by):
        route = []
        for k in range(points):
            a, b = divmod(k, minor)
            source = (a - major) % SIDE * minor + (b - minor_by) % minor
            for h in range(zh):
                route.append((source * zh + h, (k // cores * cores + h) * zh + k % cores))

        def work(shard, green_fwd, green_back):
            shard = shard.transpose(1, 0, 2).reshape(rows * blocks, orb)
            shard = lax.ppermute(shard, ("c", "zh"), transposed)
            green_fwd = lax.ppermute(green_fwd, ("c", "zh"), transposed)
            green_back = lax.ppermute(turned(high[None], green_back), ("zl", "c", "zh"), route)
            mine = spread(shard, ("y", "x"), ys * xs)
            mine = mine.reshape(ys * xs * rows * blocks, orb)
            mine, green_fwd, green_back = lax.optimization_barrier((mine, green_fwd, green_back))
            other = lax.ppermute(mine, "c", [(0, 1), (1, 0)])
            coef_mine, left_mine = left_half(mine, green_fwd, blocks)
            coef_other, left_other = left_half(other, green_fwd, blocks)
            return product(
                core[None], coef_mine, coef_other, left_mine, left_other, green_back, zl * zh, cores
            )

        return work

    works = [partner(a, b) for a in range(1, SIDE) for b in range(1, minor)]
    pairs = lax.switch(branch, works, bcoef[0], fwd_green[0, 0], back_green[0, 0])
    parts = lax.all_to_all(pairs, ("zl", "zh"), 0, 0, tiled=True)
    summed = jnp.sum(parts, axis=0)
    entries = jnp.broadcast_to(summed[:, None, :], (cores, ys * xs, blocks))
    entries = entries.reshape(cores * ys * xs, blocks)
    times = lax.all_to_all(entries, ("c", "y", "x"), 0, 0, tiled=True)
    chosen = lax.dynamic_slice_in_dim(ir_table, freq_index[own_w], 1, axis=1)
    fit = ir_fit.reshape(-1, ys, cores, xs).transpose(0, 2, 1, 3).reshape(ir_fit.shape)
    transform = jnp.sum(chosen.transpose(0, 2, 1) * fit[None], axis=1)
    result = jnp.sum(transform[:, :, None] * times[None], axis=1)
    return result[:, None, None, :]


def solution(mesh):
    sizes = {"zl": 8, "c": 2, "y": 4, "zh": 2, "x": 4}
    fine = Mesh(mesh.devices.reshape(tuple(sizes.values())), tuple(sizes))
    ka, tau = ("zl", "c"), ("y", "zh", "x")
    return jax.shard_map(
        functools.partial(shards, sizes),
        mesh=fine,
        in_specs=(
            P(ka, None, tau, None),
            P(ka, tau, None, None),
            P(ka, tau, None, None),
            P(ka),
            P(),
            P(),
            P(),
        ),
        out_specs=P(None, tau, ka, None),
        check_vma=False,
    )
```

```python
import functools

import jax
import jax.numpy as jnp
from jax import lax
from jax.experimental import pallas as pl
from jax.experimental.pallas import tpu as pltpu
from jax.sharding import Mesh
from jax.sharding import PartitionSpec as P

SIDE = 4
TILE = 16
POINTS = 16
VMEM_LIMIT = 24 * 1024 * 1024
SMALL_LIMIT = 8 * 1024 * 1024
COST = pl.CostEstimate(flops=1000, bytes_accessed=1000, transcendentals=0)


def onehot(rows, columns):
    return (rows == columns).astype(jnp.float32).astype(jnp.bfloat16)


def swap_order(blocks):
    size = TILE * blocks
    at = lax.broadcasted_iota(jnp.int32, (size, size), 0)
    source = lax.broadcasted_iota(jnp.int32, (size, size), 1)
    return onehot(at % TILE * blocks + at // TILE, source)


def ordered(order, piece_ref, group, blocks):
    size = TILE * blocks
    piece = piece_ref[pl.ds(pl.multiple_of(group * size, size), size), :]
    return jnp.dot(order, piece, preferred_element_type=jnp.float32).astype(jnp.bfloat16)


def left_kernel(piece_ref, fwd_ref, coef_ref, left_ref):
    blocks = coef_ref.shape[0]
    width = fwd_ref.shape[-1]
    order = swap_order(blocks)
    step = 3

    @pl.loop(0, coef_ref.shape[1] // TILE // step)
    def _(turn):
        coefs = []
        for part in range(step):
            group = turn * step + part
            coef = ordered(order, piece_ref, group, blocks)
            spot = pl.ds(pl.multiple_of(group * TILE, TILE), TILE)
            coef_ref[:, spot, :] = coef.reshape(blocks, TILE, width)
            coefs.append(coef)
        left = jnp.dot(
            jnp.concatenate(coefs, axis=0), fwd_ref[...], preferred_element_type=jnp.float32
        )
        left = left.astype(jnp.bfloat16).reshape(step, blocks, TILE, width)
        for part in range(step):
            group = turn * step + part
            spot = pl.ds(pl.multiple_of(group * TILE, TILE), TILE)
            left_ref[:, spot, :] = left[part]


def turn_kernel(side_ref, back_ref, out_ref):
    side = side_ref[0]
    run = 3 * TILE

    def picked(side):
        starts = [pl.multiple_of(y * 2 * run + side * run, TILE) for y in range(SIDE)]
        return jnp.concatenate([back_ref[pl.ds(at, run), :] for at in starts], axis=0)

    out_ref[...] = jnp.concatenate([picked(side), picked(1 - side)], axis=0).T


def turned(side, green_back):
    return pl.pallas_call(
        turn_kernel,
        out_shape=jax.ShapeDtypeStruct(green_back.shape, green_back.dtype),
        in_specs=[
            pl.BlockSpec(memory_space=pltpu.SMEM),
            pl.BlockSpec(memory_space=pltpu.VMEM),
        ],
        out_specs=pl.BlockSpec(memory_space=pltpu.VMEM),
        compiler_params=pltpu.CompilerParams(vmem_limit_bytes=SMALL_LIMIT),
        cost_estimate=COST,
    )(side, green_back)


def product_kernel(
    core_ref, coef_mine_ref, coef_other_ref, left_mine_ref, left_other_ref, back_t_ref, out_ref, right_ref
):
    blocks, half, width = coef_mine_ref.shape
    core = core_ref[0]
    run = 3 * TILE

    @pl.loop(0, blocks // 2)
    def _(pair):
        coefs = []
        for p in (2 * pair, 2 * pair + 1):
            coefs.append(jnp.concatenate([coef_mine_ref[p], coef_other_ref[p]], axis=0))
        right = jnp.dot(
            back_t_ref[...], jnp.concatenate(coefs, axis=1), preferred_element_type=jnp.float32
        )
        right = right.astype(jnp.bfloat16)
        right_ref[2 * pair] = right[:, :width]
        right_ref[2 * pair + 1] = right[:, width:]

    size = TILE * blocks
    gram = jnp.zeros((size, size), jnp.float32)
    for side, lefts in ((core, left_mine_ref), (1 - core, left_other_ref)):
        for y in range(SIDE):
            left_parts, right_parts = [], []
            for part in range(run // TILE):
                at = y * run + part * TILE
                natural = pl.multiple_of(y * 2 * run + side * run + part * TILE, TILE)
                left_parts.append(lefts[:, at : at + TILE, :].reshape(size, width))
                right_parts.append(right_ref[:, pl.ds(natural, TILE), :].reshape(size, width))
            gram += lax.dot_general(
                jnp.concatenate(left_parts, axis=1),
                jnp.concatenate(right_parts, axis=1),
                (((1,), (1,)), ((), ())),
                preferred_element_type=jnp.float32,
            )
    row = lax.broadcasted_iota(jnp.int32, (size, size), 0) % TILE
    column = lax.broadcasted_iota(jnp.int32, (size, size), 1) % TILE
    gram = jnp.where(row == column, gram, 0.0)
    gram = jnp.sum(gram.reshape(blocks, TILE, size), axis=1)
    at = lax.broadcasted_iota(jnp.int32, (size, blocks), 0) // TILE
    which = lax.broadcasted_iota(jnp.int32, (size, blocks), 1)
    pick = (at == which).astype(jnp.float32)
    polar = jnp.dot(gram, pick, precision=lax.Precision.HIGHEST, preferred_element_type=jnp.float32)
    polar = polar * (-1.0 / POINTS)
    _, cores, _ = out_ref.shape
    for p in range(blocks):
        for copy in range(out_ref.shape[0] * cores // blocks):
            place = p // cores * (out_ref.shape[0] * cores // blocks) + copy
            out_ref[place, p % cores : p % cores + 1, :] = polar[p : p + 1, :]


def left_half(piece, green_fwd, blocks):
    width = green_fwd.shape[-1]
    shape = jax.ShapeDtypeStruct((blocks, piece.shape[0] // blocks, width), jnp.bfloat16)
    return pl.pallas_call(
        left_kernel,
        out_shape=(shape, shape),
        in_specs=[pl.BlockSpec(memory_space=pltpu.VMEM)] * 2,
        out_specs=[pl.BlockSpec(memory_space=pltpu.VMEM)] * 2,
        compiler_params=pltpu.CompilerParams(vmem_limit_bytes=VMEM_LIMIT),
        cost_estimate=COST,
    )(piece, green_fwd)


def product(coef_mine, coef_other, left_mine, left_other, green_back, core, receivers, cores):
    blocks, half, width = coef_mine.shape
    return pl.pallas_call(
        product_kernel,
        out_shape=jax.ShapeDtypeStruct((receivers, cores, blocks), jnp.float32),
        in_specs=[pl.BlockSpec(memory_space=pltpu.SMEM)]
        + [pl.BlockSpec(memory_space=pltpu.VMEM)] * 5,
        out_specs=pl.BlockSpec(memory_space=pltpu.VMEM),
        scratch_shapes=[
            pltpu.VMEM((blocks, width, width), jnp.bfloat16),
        ],
        compiler_params=pltpu.CompilerParams(vmem_limit_bytes=VMEM_LIMIT),
        cost_estimate=COST,
    )(core, coef_mine, coef_other, left_mine, left_other, green_back)


def settle_kernel(block_ref, out_ref):
    out_ref[...] = block_ref[...]


def settled(block):
    return pl.pallas_call(
        settle_kernel,
        out_shape=jax.ShapeDtypeStruct(block.shape, block.dtype),
        in_specs=[pl.BlockSpec(memory_space=pltpu.VMEM)],
        out_specs=pl.BlockSpec(memory_space=pltpu.VMEM),
        compiler_params=pltpu.CompilerParams(vmem_limit_bytes=SMALL_LIMIT),
        cost_estimate=pl.CostEstimate(
            flops=50_000_000_000, bytes_accessed=2_500_000, transcendentals=0
        ),
    )(block)


def spread(block, axes, count):
    copies = jnp.broadcast_to(block[None], (count,) + block.shape)
    return lax.all_to_all(copies, axes, 0, 0, tiled=True)


def shards(sizes, bcoef, fwd_green, back_green, kmq, ir_table, ir_fit, freq_index):
    zl, cores, ys, zh, xs = (sizes[name] for name in ("zl", "c", "y", "zh", "x"))
    blocks, rows, orb = bcoef.shape[1:]
    points = zl * cores
    minor = points // SIDE
    core = lax.axis_index("c")
    high = lax.axis_index("zh")
    low = lax.axis_index("zl")
    here_y, here_x = lax.axis_index("y"), lax.axis_index("x")

    own_w = (here_y * zh + high) * xs + here_x
    own_k = low * cores + core
    target = kmq[0]
    major_shift = ((own_k >> 2) - (target >> 2)) & 3
    minor_shift = ((own_k & 3) - (target & 3)) & 3
    branch = (major_shift - 1) * (minor - 1) + minor_shift - 1

    transposed = [(c * zh + h, h * zh + c) for c in range(cores) for h in range(zh)]

    def partner(major, minor_by):
        route = []
        for k in range(points):
            a, b = divmod(k, minor)
            source = (a - major) % SIDE * minor + (b - minor_by) % minor
            for h in range(zh):
                route.append((source * zh + h, (k // cores * cores + h) * zh + k % cores))

        def work(shard, green_fwd, green_back):
            shard = shard.transpose(1, 0, 2).reshape(rows * blocks, orb)
            shard = lax.ppermute(shard, ("c", "zh"), transposed)
            green_fwd = lax.ppermute(green_fwd, ("c", "zh"), transposed)
            green_back = lax.ppermute(green_back, ("zl", "c", "zh"), route)
            mine = lax.cond(
                target >= 0,
                lambda block: spread(block, ("y", "x"), ys * xs),
                lambda block: jnp.zeros((ys * xs,) + block.shape, block.dtype),
                settled(shard),
            )
            mine = mine.reshape(ys * xs * rows * blocks, orb)
            return mine, green_fwd, green_back

        return work

    works = [partner(a, b) for a in range(1, SIDE) for b in range(1, minor)]
    mine, green_fwd, green_back = lax.switch(
        branch, works, bcoef[0], fwd_green[0, 0], back_green[0, 0]
    )
    other = lax.ppermute(mine, "c", [(0, 1), (1, 0)])
    coef_mine, left_mine = left_half(mine, green_fwd, blocks)
    green_back = turned(core[None], green_back)
    coef_other, left_other = left_half(other, green_fwd, blocks)
    pairs = product(coef_mine, coef_other, left_mine, left_other, green_back, core[None], zl * zh, cores)
    parts = lax.all_to_all(pairs, ("zl", "zh"), 0, 0, tiled=True)
    summed = jnp.sum(parts, axis=0)
    entries = jnp.broadcast_to(summed[:, None, :], (cores, ys * xs, blocks))
    entries = entries.reshape(cores * ys * xs, blocks)
    times = lax.all_to_all(entries, ("c", "y", "x"), 0, 0, tiled=True)
    chosen = lax.dynamic_slice_in_dim(ir_table, freq_index[own_w], 1, axis=1)
    fit = ir_fit.reshape(-1, ys, cores, xs).transpose(0, 2, 1, 3).reshape(ir_fit.shape)
    transform = jnp.sum(chosen.transpose(0, 2, 1) * fit[None], axis=1)
    result = jnp.sum(transform[:, :, None] * times[None], axis=1)
    return result[:, None, None, :]


def solution(mesh):
    sizes = {"zl": 8, "c": 2, "y": 4, "zh": 2, "x": 4}
    fine = Mesh(mesh.devices.reshape(tuple(sizes.values())), tuple(sizes))
    ka, tau = ("zl", "c"), ("y", "zh", "x")
    return jax.shard_map(
        functools.partial(shards, sizes),
        mesh=fine,
        in_specs=(
            P(ka, None, tau, None),
            P(ka, tau, None, None),
            P(ka, tau, None, None),
            P(ka),
            P(),
            P(),
            P(),
        ),
        out_specs=P(None, tau, ka, None),
        check_vma=False,
    )
```

```python
import functools

import jax
import jax.numpy as jnp
import numpy as np
from jax import lax
from jax.experimental import pallas as pl
from jax.experimental.pallas import tpu as pltpu
from jax.sharding import Mesh
from jax.sharding import PartitionSpec as P

SIDE = 4
TILE = 16
POINTS = 16
VMEM_LIMIT = 24 * 1024 * 1024
SMALL_LIMIT = 8 * 1024 * 1024
COST = pl.CostEstimate(flops=1000, bytes_accessed=1000, transcendentals=0)


def onehot(rows, columns):
    return (rows == columns).astype(jnp.float32).astype(jnp.bfloat16)


def swap_order(blocks):
    size = TILE * blocks
    at = lax.broadcasted_iota(jnp.int32, (size, size), 0)
    source = lax.broadcasted_iota(jnp.int32, (size, size), 1)
    return onehot(at % TILE * blocks + at // TILE, source)


def ordered(order, piece_ref, group, blocks):
    size = TILE * blocks
    piece = piece_ref[pl.ds(pl.multiple_of(group * size, size), size), :]
    return jnp.dot(order, piece, preferred_element_type=jnp.float32).astype(jnp.bfloat16)


def left_turn(order, piece_ref, fwd_ref, coef_ref, left_ref, turn, step):
    blocks = coef_ref.shape[0]
    width = fwd_ref.shape[-1]
    coefs = []
    for part in range(step):
        group = turn * step + part
        coef = ordered(order, piece_ref, group, blocks)
        spot = pl.ds(pl.multiple_of(group * TILE, TILE), TILE)
        coef_ref[:, spot, :] = coef.reshape(blocks, TILE, width)
        coefs.append(coef)
    left = jnp.dot(jnp.concatenate(coefs, axis=0), fwd_ref[...], preferred_element_type=jnp.float32)
    left = left.astype(jnp.bfloat16).reshape(step, blocks * TILE, width)
    for part in range(step):
        group = turn * step + part
        left_ref[:, pl.ds(pl.multiple_of(group * width, width), width)] = left[part]


def first_kernel(
    core_ref, piece_hbm, fwd_hbm, back_hbm, rows_hbm, coef_ref, left_ref, fwd_ref, back_t_ref, piece_ref, back_ref, rows_ref, sems
):
    blocks = coef_ref.shape[0]
    order = swap_order(blocks)
    step = 3
    turns = coef_ref.shape[1] // TILE // step
    size = step * TILE * blocks

    def piece_copy(turn):
        spot = pl.ds(pl.multiple_of(turn * size, size), size)
        return pltpu.make_async_copy(piece_hbm.at[spot], piece_ref.at[spot], sems.at[turn])

    fwd_copy = pltpu.make_async_copy(fwd_hbm, fwd_ref, sems.at[turns])
    back_copy = pltpu.make_async_copy(back_hbm, back_ref, sems.at[turns + 1])
    rows_copy = pltpu.make_async_copy(rows_hbm.at[core_ref[0]], rows_ref, sems.at[turns + 2])
    piece_copy(0).start()
    fwd_copy.start()
    for turn in range(1, turns):
        piece_copy(turn).start()
    back_copy.start()
    rows_copy.start()
    fwd_copy.wait()

    @pl.loop(0, turns)
    def _(turn):
        piece_copy(turn).wait()
        left_turn(order, piece_ref, fwd_ref, coef_ref, left_ref, turn, step)

    back_copy.wait()
    rows_copy.wait()
    rows = rows_ref[...]
    back = jnp.dot(rows, back_ref[...], preferred_element_type=jnp.float32).astype(jnp.bfloat16)
    back_t = lax.dot_general(
        rows, back, (((1,), (1,)), ((), ())), preferred_element_type=jnp.float32
    )
    back_t_ref[...] = back_t.astype(jnp.bfloat16)


def left_kernel(piece_ref, fwd_ref, coef_ref, left_ref):
    order = swap_order(coef_ref.shape[0])
    step = 3

    @pl.loop(0, coef_ref.shape[1] // TILE // step)
    def _(turn):
        left_turn(order, piece_ref, fwd_ref, coef_ref, left_ref, turn, step)


def product_kernel(
    coef_mine_ref, coef_other_ref, left_mine_ref, left_other_ref, back_t_ref, out_ref, right_ref
):
    blocks, half, width = coef_mine_ref.shape
    per_side = half // TILE

    @pl.loop(0, blocks // 2, unroll=4)
    def _(pair):
        coefs = []
        for p in (2 * pair, 2 * pair + 1):
            coefs.append(jnp.concatenate([coef_mine_ref[p], coef_other_ref[p]], axis=0))
        right = jnp.dot(
            back_t_ref[...], jnp.concatenate(coefs, axis=1), preferred_element_type=jnp.float32
        )
        right = right.astype(jnp.bfloat16)
        for inner in range(2):
            rows = pl.ds(pl.multiple_of((2 * pair + inner) * TILE, TILE), TILE)
            for block in range(2 * per_side):
                at = block % per_side * width
                right_ref[block // per_side, rows, at : at + width] = right[
                    block * TILE : (block + 1) * TILE, inner * width : (inner + 1) * width
                ]

    size = TILE * blocks
    gram = jnp.zeros((size, size), jnp.float32)
    for side, lefts in enumerate((left_mine_ref, left_other_ref)):
        gram += lax.dot_general(
            lefts[...], right_ref[side], (((1,), (1,)), ((), ())), preferred_element_type=jnp.float32
        )
    row = lax.broadcasted_iota(jnp.int32, (size, size), 0) % TILE
    column = lax.broadcasted_iota(jnp.int32, (size, size), 1) % TILE
    gram = jnp.where(row == column, gram, 0.0)
    gram = jnp.sum(gram.reshape(blocks, TILE, size), axis=1)
    at = lax.broadcasted_iota(jnp.int32, (size, blocks), 0) // TILE
    which = lax.broadcasted_iota(jnp.int32, (size, blocks), 1)
    pick = (at == which).astype(jnp.float32)
    polar = jnp.dot(gram, pick, precision=lax.Precision.HIGHEST, preferred_element_type=jnp.float32)
    polar = polar * (-1.0 / POINTS)
    _, cores, _ = out_ref.shape
    for p in range(blocks):
        for copy in range(out_ref.shape[0] * cores // blocks):
            place = p // cores * (out_ref.shape[0] * cores // blocks) + copy
            out_ref[place, p % cores : p % cores + 1, :] = polar[p : p + 1, :]


def half_shapes(piece, blocks):
    width = piece.shape[-1]
    half = piece.shape[0] // blocks
    coef = jax.ShapeDtypeStruct((blocks, half, width), jnp.bfloat16)
    left = jax.ShapeDtypeStruct((blocks * TILE, half // TILE * width), jnp.bfloat16)
    return coef, left


def first_half(core, piece, green_fwd, green_back, row_orders, blocks):
    width = green_fwd.shape[-1]
    square = jax.ShapeDtypeStruct((width, width), jnp.bfloat16)
    return pl.pallas_call(
        first_kernel,
        out_shape=half_shapes(piece, blocks) + (square, square),
        in_specs=[pl.BlockSpec(memory_space=pltpu.SMEM)] + [pl.BlockSpec(memory_space=pl.ANY)] * 4,
        out_specs=[pl.BlockSpec(memory_space=pltpu.VMEM)] * 4,
        scratch_shapes=[
            pltpu.VMEM(piece.shape, jnp.bfloat16),
            pltpu.VMEM((width, width), jnp.bfloat16),
            pltpu.VMEM((width, width), jnp.bfloat16),
            pltpu.SemaphoreType.DMA((SIDE + 3,)),
        ],
        compiler_params=pltpu.CompilerParams(vmem_limit_bytes=VMEM_LIMIT),
        cost_estimate=COST,
    )(core, piece, green_fwd, green_back, row_orders)


def second_half(piece, green_fwd, blocks):
    return pl.pallas_call(
        left_kernel,
        out_shape=half_shapes(piece, blocks),
        in_specs=[pl.BlockSpec(memory_space=pltpu.VMEM)] * 2,
        out_specs=[pl.BlockSpec(memory_space=pltpu.VMEM)] * 2,
        compiler_params=pltpu.CompilerParams(vmem_limit_bytes=VMEM_LIMIT),
        cost_estimate=COST,
    )(piece, green_fwd)


def product(coef_mine, coef_other, left_mine, left_other, back_t, receivers, cores):
    blocks, half, width = coef_mine.shape
    return pl.pallas_call(
        product_kernel,
        out_shape=jax.ShapeDtypeStruct((receivers, cores, blocks), jnp.float32),
        in_specs=[pl.BlockSpec(memory_space=pltpu.VMEM)] * 5,
        out_specs=pl.BlockSpec(memory_space=pltpu.VMEM),
        scratch_shapes=[
            pltpu.VMEM((2, blocks * TILE, half // TILE * width), jnp.bfloat16),
        ],
        compiler_params=pltpu.CompilerParams(vmem_limit_bytes=VMEM_LIMIT),
        cost_estimate=COST,
    )(coef_mine, coef_other, left_mine, left_other, back_t)


def settle_kernel(block_ref, out_ref):
    out_ref[...] = block_ref[...]


def settled(block):
    return pl.pallas_call(
        settle_kernel,
        out_shape=jax.ShapeDtypeStruct(block.shape, block.dtype),
        in_specs=[pl.BlockSpec(memory_space=pltpu.VMEM)],
        out_specs=pl.BlockSpec(memory_space=pltpu.VMEM),
        compiler_params=pltpu.CompilerParams(vmem_limit_bytes=SMALL_LIMIT),
        cost_estimate=pl.CostEstimate(
            flops=50_000_000_000, bytes_accessed=2_500_000, transcendentals=0
        ),
    )(block)


def spread(block, phases):
    for groups in phases:
        count = len(groups[0])
        copies = jnp.broadcast_to(block[None], (count,) + block.shape)
        block = lax.all_to_all(
            copies, ("c", "y", "x"), 0, 0, axis_index_groups=groups, tiled=True
        ).reshape(count * block.shape[0], block.shape[1])
    return block


def spread_phases(cores, ys, xs):
    def index(c, y, x):
        return (c * ys + y) * xs + x

    along_y = [[[index(c, y, x) for y in range(ys)] for x in range(xs)] for c in range(cores)]
    along_x = [[[index(c, y, x) for x in range(xs)] for y in range(ys)] for c in range(cores)]
    return along_y[0] + along_x[1], along_x[0] + along_y[1]


def row_orders_of(cores, ys, xs, rows):
    size = cores * ys * xs * rows
    half = size // cores
    orders = np.zeros((cores, size, size), np.float32)
    for core in range(cores):
        for at in range(size):
            bit = core if at < half else 1 - core
            outer, inner, row = at % half // (xs * rows), at // rows % xs, at % rows
            y, x = (outer, inner) if bit else (inner, outer)
            orders[core, at, ((y * cores + bit) * xs + x) * rows + row] = 1.0
    return jnp.asarray(orders, jnp.bfloat16)


def shards(sizes, bcoef, fwd_green, back_green, kmq, ir_table, ir_fit, freq_index):
    zl, cores, ys, zh, xs = (sizes[name] for name in ("zl", "c", "y", "zh", "x"))
    blocks, rows, orb = bcoef.shape[1:]
    points = zl * cores
    minor = points // SIDE
    core = lax.axis_index("c")
    high = lax.axis_index("zh")
    low = lax.axis_index("zl")
    here_y, here_x = lax.axis_index("y"), lax.axis_index("x")

    own_w = (here_y * zh + high) * xs + here_x
    own_k = low * cores + core
    target = kmq[0]
    major_shift = ((own_k >> 2) - (target >> 2)) & 3
    minor_shift = ((own_k & 3) - (target & 3)) & 3
    branch = (major_shift - 1) * (minor - 1) + minor_shift - 1

    phases = spread_phases(cores, ys, xs)
    transposed = [(c * zh + h, h * zh + c) for c in range(cores) for h in range(zh)]

    def partner(major, minor_by):
        route = []
        for k in range(points):
            a, b = divmod(k, minor)
            source = (a - major) % SIDE * minor + (b - minor_by) % minor
            for h in range(zh):
                route.append((source * zh + h, (k // cores * cores + h) * zh + k % cores))

        def work(shard, green_fwd, green_back):
            shard = shard.transpose(1, 0, 2).reshape(rows * blocks, orb)
            shard = lax.ppermute(shard, ("c", "zh"), transposed)
            green_fwd = lax.ppermute(green_fwd, ("c", "zh"), transposed)
            green_back = lax.ppermute(green_back, ("zl", "c", "zh"), route)
            mine = lax.cond(
                target >= 0,
                lambda block: spread(block, phases),
                lambda block: jnp.zeros((ys * xs * block.shape[0], block.shape[1]), block.dtype),
                settled(shard),
            )
            return mine, green_fwd, green_back

        return work

    works = [partner(a, b) for a in range(1, SIDE) for b in range(1, minor)]
    mine, green_fwd, green_back = lax.switch(
        branch, works, bcoef[0], fwd_green[0, 0], back_green[0, 0]
    )
    other = lax.ppermute(mine, "c", [(0, 1), (1, 0)])
    row_orders = row_orders_of(cores, ys, xs, rows)
    coef_mine, left_mine, green_fwd, back_t = first_half(
        core[None], mine, green_fwd, green_back, row_orders, blocks
    )
    coef_other, left_other = second_half(other, green_fwd, blocks)
    pairs = product(coef_mine, coef_other, left_mine, left_other, back_t, zl * zh, cores)
    parts = lax.all_to_all(pairs, ("zl", "zh"), 0, 0, tiled=True)
    summed = jnp.sum(parts, axis=0)
    entries = jnp.broadcast_to(summed[:, None, :], (cores, ys * xs, blocks))
    entries = entries.reshape(cores * ys * xs, blocks)
    times = lax.all_to_all(entries, ("c", "y", "x"), 0, 0, tiled=True)
    chosen = lax.dynamic_slice_in_dim(ir_table, freq_index[own_w], 1, axis=1)
    fit = ir_fit.reshape(-1, ys, cores, xs).transpose(0, 2, 1, 3).reshape(ir_fit.shape)
    transform = jnp.sum(chosen.transpose(0, 2, 1) * fit[None], axis=1)
    result = jnp.sum(transform[:, :, None] * times[None], axis=1)
    return result[:, None, None, :]


def solution(mesh):
    sizes = {"zl": 8, "c": 2, "y": 4, "zh": 2, "x": 4}
    fine = Mesh(mesh.devices.reshape(tuple(sizes.values())), tuple(sizes))
    ka, tau = ("zl", "c"), ("y", "zh", "x")
    return jax.shard_map(
        functools.partial(shards, sizes),
        mesh=fine,
        in_specs=(
            P(ka, None, tau, None),
            P(ka, tau, None, None),
            P(ka, tau, None, None),
            P(ka),
            P(),
            P(),
            P(),
        ),
        out_specs=P(None, tau, ka, None),
        check_vma=False,
    )
```

```python
import functools

import jax
import jax.numpy as jnp
from jax import lax
from jax.experimental import pallas as pl
from jax.experimental.pallas import tpu as pltpu
from jax.sharding import Mesh
from jax.sharding import PartitionSpec as P

SIDE = 4
ROWS = 12
STEP = 4
TILE = 16
POINTS = 16
FIRST_LIMIT = 10 * 1024 * 1024
PRODUCT_LIMIT = 14 * 1024 * 1024
SMALL_LIMIT = 8 * 1024 * 1024
COST = pl.CostEstimate(flops=1000, bytes_accessed=1000, transcendentals=0)


def onehot(rows, columns):
    return (rows == columns).astype(jnp.float32).astype(jnp.bfloat16)


def swap_order(blocks):
    size = TILE * blocks
    at = lax.broadcasted_iota(jnp.int32, (size, size), 0)
    source = lax.broadcasted_iota(jnp.int32, (size, size), 1)
    return onehot(at % TILE * blocks + at // TILE, source)


def row_order(size, lane, odd):
    at = lax.broadcasted_iota(jnp.int32, (size, 1), 0)
    side = (at >= size // 2).astype(jnp.int32)
    here = lane ^ side
    rest = at - side * (size // 2)
    shard = (rest * 171) >> 11
    row = rest - shard * ROWS
    outer, inner = shard >> 2, shard & 3
    y = jnp.where(here == 1, outer, inner)
    x = jnp.where(here == 1, inner, outer)
    bit = here ^ ((x + y) & 1) ^ odd
    return onehot(((y * 2 + bit) * SIDE + x) * ROWS + row, lax.broadcasted_iota(jnp.int32, (size, size), 1))


def left_turn(order, piece_ref, fwd_ref, coef_ref, left_ref, turn, step):
    blocks = coef_ref.shape[0]
    width = fwd_ref.shape[-1]
    size = TILE * blocks
    pieces = [
        piece_ref[pl.ds(pl.multiple_of((turn * step + part) * size, size), size), :]
        for part in range(step)
    ]
    wide = jnp.dot(order, jnp.concatenate(pieces, axis=1), preferred_element_type=jnp.float32)
    wide = wide.astype(jnp.bfloat16)
    coefs = []
    for part in range(step):
        group = turn * step + part
        coef = wide[:, part * width : (part + 1) * width]
        spot = pl.ds(pl.multiple_of(group * TILE, TILE), TILE)
        coef_ref[:, spot, :] = coef.reshape(blocks, TILE, width)
        coefs.append(coef)
    left = jnp.dot(jnp.concatenate(coefs, axis=0), fwd_ref[...], preferred_element_type=jnp.float32)
    left = left.astype(jnp.bfloat16).reshape(step, blocks * TILE, width)
    for part in range(step):
        group = turn * step + part
        left_ref[:, pl.ds(pl.multiple_of(group * width, width), width)] = left[part]


def first_kernel(
    lane_ref, odd_ref, piece_hbm, fwd_hbm, back_hbm, coef_ref, left_ref, fwd_ref, back_t_ref, piece_ref, back_ref, sems
):
    blocks = coef_ref.shape[0]
    order = swap_order(blocks)
    step = STEP
    turns = coef_ref.shape[1] // TILE // step
    size = step * TILE * blocks

    def piece_copy(turn):
        spot = pl.ds(pl.multiple_of(turn * size, size), size)
        return pltpu.make_async_copy(piece_hbm.at[spot], piece_ref.at[spot], sems.at[turn])

    fwd_copy = pltpu.make_async_copy(fwd_hbm, fwd_ref, sems.at[turns])
    back_copy = pltpu.make_async_copy(back_hbm, back_ref, sems.at[turns + 1])
    piece_copy(0).start()
    fwd_copy.start()
    for turn in range(1, turns):
        piece_copy(turn).start()
    back_copy.start()
    fwd_copy.wait()

    @pl.loop(0, turns)
    def _(turn):
        piece_copy(turn).wait()
        left_turn(order, piece_ref, fwd_ref, coef_ref, left_ref, turn, step)

    back_copy.wait()
    rows = row_order(back_ref.shape[0], lane_ref[0], odd_ref[0])
    back = jnp.dot(rows, back_ref[...], preferred_element_type=jnp.float32).astype(jnp.bfloat16)
    back_t = lax.dot_general(
        rows, back, (((1,), (1,)), ((), ())), preferred_element_type=jnp.float32
    )
    back_t_ref[...] = back_t.astype(jnp.bfloat16)


def left_kernel(piece_ref, fwd_ref, coef_ref, left_ref):
    order = swap_order(coef_ref.shape[0])
    step = STEP

    @pl.loop(0, coef_ref.shape[1] // TILE // step)
    def _(turn):
        left_turn(order, piece_ref, fwd_ref, coef_ref, left_ref, turn, step)


def product_kernel(
    coef_mine_ref, coef_other_ref, left_mine_ref, left_other_ref, back_t_ref, out_ref, right_ref
):
    blocks, half, width = coef_mine_ref.shape
    per_side = half // TILE

    @pl.loop(0, blocks // 2, unroll=4)
    def _(pair):
        coefs = []
        for p in (2 * pair, 2 * pair + 1):
            coefs.append(jnp.concatenate([coef_mine_ref[p], coef_other_ref[p]], axis=0))
        right = jnp.dot(
            back_t_ref[...], jnp.concatenate(coefs, axis=1), preferred_element_type=jnp.float32
        )
        right = right.astype(jnp.bfloat16)
        for inner in range(2):
            rows = pl.ds(pl.multiple_of((2 * pair + inner) * TILE, TILE), TILE)
            for block in range(2 * per_side):
                at = block % per_side * width
                right_ref[block // per_side, rows, at : at + width] = right[
                    block * TILE : (block + 1) * TILE, inner * width : (inner + 1) * width
                ]

    size = TILE * blocks
    gram = jnp.zeros((size, size), jnp.float32)
    for side, lefts in enumerate((left_mine_ref, left_other_ref)):
        gram += lax.dot_general(
            lefts[...], right_ref[side], (((1,), (1,)), ((), ())), preferred_element_type=jnp.float32
        )
    row = lax.broadcasted_iota(jnp.int32, (size, size), 0) % TILE
    column = lax.broadcasted_iota(jnp.int32, (size, size), 1) % TILE
    gram = jnp.where(row == column, gram, 0.0)
    gram = jnp.sum(gram.reshape(blocks, TILE, size), axis=1)
    at = lax.broadcasted_iota(jnp.int32, (size, blocks), 0) // TILE
    which = lax.broadcasted_iota(jnp.int32, (size, blocks), 1)
    pick = (at == which).astype(jnp.float32)
    polar = jnp.dot(gram, pick, precision=lax.Precision.HIGHEST, preferred_element_type=jnp.float32)
    polar = polar * (-1.0 / POINTS)
    _, cores, _ = out_ref.shape
    for p in range(blocks):
        for copy in range(out_ref.shape[0] * cores // blocks):
            place = p // cores * (out_ref.shape[0] * cores // blocks) + copy
            out_ref[place, p % cores : p % cores + 1, :] = polar[p : p + 1, :]


def half_shapes(piece, blocks):
    width = piece.shape[-1]
    half = piece.shape[0] // blocks
    coef = jax.ShapeDtypeStruct((blocks, half, width), jnp.bfloat16)
    left = jax.ShapeDtypeStruct((blocks * TILE, half // TILE * width), jnp.bfloat16)
    return coef, left


def first_half(lane, odd, piece, green_fwd, green_back, blocks):
    width = green_fwd.shape[-1]
    square = jax.ShapeDtypeStruct((width, width), jnp.bfloat16)
    return pl.pallas_call(
        first_kernel,
        out_shape=half_shapes(piece, blocks) + (square, square),
        in_specs=[pl.BlockSpec(memory_space=pltpu.SMEM)] * 2
        + [pl.BlockSpec(memory_space=pl.ANY)] * 3,
        out_specs=[pl.BlockSpec(memory_space=pltpu.VMEM)] * 4,
        scratch_shapes=[
            pltpu.VMEM(piece.shape, jnp.bfloat16),
            pltpu.VMEM((width, width), jnp.bfloat16),
            pltpu.SemaphoreType.DMA((piece.shape[0] // (STEP * TILE * blocks) + 2,)),
        ],
        compiler_params=pltpu.CompilerParams(vmem_limit_bytes=FIRST_LIMIT),
        cost_estimate=COST,
    )(lane, odd, piece, green_fwd, green_back)


def second_half(piece, green_fwd, blocks):
    return pl.pallas_call(
        left_kernel,
        out_shape=half_shapes(piece, blocks),
        in_specs=[pl.BlockSpec(memory_space=pltpu.VMEM)] * 2,
        out_specs=[pl.BlockSpec(memory_space=pltpu.VMEM)] * 2,
        compiler_params=pltpu.CompilerParams(vmem_limit_bytes=SMALL_LIMIT),
        cost_estimate=COST,
    )(piece, green_fwd)


def product(coef_mine, coef_other, left_mine, left_other, back_t, receivers, cores):
    blocks, half, width = coef_mine.shape
    return pl.pallas_call(
        product_kernel,
        out_shape=jax.ShapeDtypeStruct((receivers, cores, blocks), jnp.float32),
        in_specs=[pl.BlockSpec(memory_space=pltpu.VMEM)] * 5,
        out_specs=pl.BlockSpec(memory_space=pltpu.VMEM),
        scratch_shapes=[
            pltpu.VMEM((2, blocks * TILE, half // TILE * width), jnp.bfloat16),
        ],
        compiler_params=pltpu.CompilerParams(vmem_limit_bytes=PRODUCT_LIMIT),
        cost_estimate=COST,
    )(coef_mine, coef_other, left_mine, left_other, back_t)


def settle_kernel(block_ref, out_ref):
    out_ref[...] = block_ref[...]


def settled(block):
    return pl.pallas_call(
        settle_kernel,
        out_shape=jax.ShapeDtypeStruct(block.shape, block.dtype),
        in_specs=[pl.BlockSpec(memory_space=pltpu.VMEM)],
        out_specs=pl.BlockSpec(memory_space=pltpu.VMEM),
        compiler_params=pltpu.CompilerParams(vmem_limit_bytes=SMALL_LIMIT),
        cost_estimate=pl.CostEstimate(
            flops=50_000_000_000, bytes_accessed=2_500_000, transcendentals=0
        ),
    )(block)


def spread(block, phases):
    for groups in phases:
        count = len(groups[0])
        copies = jnp.broadcast_to(block[None], (count,) + block.shape)
        block = lax.all_to_all(
            copies, ("c", "y", "x"), 0, 0, axis_index_groups=groups, tiled=True
        ).reshape(count * block.shape[0], block.shape[1])
    return block


def spread_phases(cores, ys, xs):
    def index(lane, y, x):
        return ((lane ^ (x + y) & 1) * ys + y) * xs + x

    along_y = [[[index(c, y, x) for y in range(ys)] for x in range(xs)] for c in range(cores)]
    along_x = [[[index(c, y, x) for x in range(xs)] for y in range(ys)] for c in range(cores)]
    return along_y[0] + along_x[1], along_x[0] + along_y[1]


def shards(sizes, bcoef, fwd_green, back_green, kmq, ir_table, ir_fit, freq_index):
    zl, cores, ys, zh, xs = (sizes[name] for name in ("zl", "c", "y", "zh", "x"))
    blocks, rows, orb = bcoef.shape[1:]
    points = zl * cores
    minor = points // SIDE
    core = lax.axis_index("c")
    high = lax.axis_index("zh")
    low = lax.axis_index("zl")
    here_y, here_x = lax.axis_index("y"), lax.axis_index("x")

    own_w = (here_y * zh + high) * xs + here_x
    own_k = low * cores + core
    target = kmq[0]
    major_shift = ((own_k >> 2) - (target >> 2)) & 3
    minor_shift = ((own_k & 3) - (target & 3)) & 3
    branch = (major_shift - 1) * (minor - 1) + minor_shift - 1

    phases = spread_phases(cores, ys, xs)
    odd = low & 1
    swapped = [
        ((z * cores + c) * zh + h, (z * cores + (h ^ z & 1)) * zh + (c ^ z & 1))
        for z in range(zl)
        for c in range(cores)
        for h in range(zh)
    ]
    columns = [
        [(z * cores + (half ^ z & 1)) * zh + h for z in range(zl) for h in range(zh)]
        for half in range(cores)
    ]

    def partner(major, minor_by):
        route = []
        for k in range(points):
            a, b = divmod(k, minor)
            source = (a - major) % SIDE * minor + (b - minor_by) % minor
            for h in range(zh):
                z, odd = k // cores, k // cores & 1
                route.append((source * zh + h, (z * cores + (h ^ odd)) * zh + (k % cores ^ odd)))

        def work(shard, green_fwd, green_back):
            shard = shard.transpose(1, 0, 2).reshape(rows * blocks, orb)
            shard = lax.ppermute(shard, ("zl", "c", "zh"), swapped)
            green_fwd = lax.ppermute(green_fwd, ("zl", "c", "zh"), swapped)
            green_back = lax.ppermute(green_back, ("zl", "c", "zh"), route)
            mine = lax.cond(
                target >= 0,
                lambda block: spread(block, phases),
                lambda block: jnp.zeros((ys * xs * block.shape[0], block.shape[1]), block.dtype),
                settled(shard),
            )
            return mine, green_fwd, green_back

        return work

    works = [partner(a, b) for a in range(1, SIDE) for b in range(1, minor)]
    mine, green_fwd, green_back = lax.switch(
        branch, works, bcoef[0], fwd_green[0, 0], back_green[0, 0]
    )
    mine, own_w, odd, is_odd, lane = lax.optimization_barrier(
        (mine, own_w.astype(jnp.uint32), odd, odd == 1, core ^ (here_x + here_y) & 1)
    )
    other = lax.ppermute(mine, "c", [(0, 1), (1, 0)])
    coef_mine, left_mine, green_fwd, back_t = first_half(
        lane[None], odd[None], mine, green_fwd, green_back, blocks
    )
    coef_other, left_other = second_half(other, green_fwd, blocks)
    pairs = product(coef_mine, coef_other, left_mine, left_other, back_t, zl * zh, cores)
    pairs, ir_table, ir_fit, freq_index = lax.optimization_barrier(
        (pairs, ir_table, ir_fit, freq_index)
    )
    parts = lax.all_to_all(
        pairs, ("zl", "c", "zh"), 0, 0, axis_index_groups=columns, tiled=True
    )
    summed = jnp.sum(parts, axis=0)
    entries = jnp.broadcast_to(summed[:, None, :], (cores, ys * xs, blocks))
    entries = entries.reshape(cores * ys * xs, blocks)
    times = lax.all_to_all(entries, ("c", "y", "x"), 0, 0, tiled=True)
    chosen = lax.dynamic_slice_in_dim(ir_table, lax.dynamic_slice(freq_index, (own_w,), (1,))[0], 1, axis=1)
    fit = ir_fit.reshape(-1, ys, cores, xs).transpose(0, 2, 1, 3)
    fit = jnp.where(is_odd, fit[:, ::-1], fit).reshape(ir_fit.shape)
    transform = jnp.sum(chosen.transpose(0, 2, 1) * fit[None], axis=1)
    result = jnp.sum(transform[:, :, None] * times[None], axis=1)
    return result[:, None, None, :]


def solution(mesh):
    sizes = {"zl": 8, "c": 2, "y": 4, "zh": 2, "x": 4}
    fine = Mesh(mesh.devices.reshape(tuple(sizes.values())), tuple(sizes))
    ka, tau = ("zl", "c"), ("y", "zh", "x")
    return jax.shard_map(
        functools.partial(shards, sizes),
        mesh=fine,
        in_specs=(
            P(ka, None, tau, None),
            P(ka, tau, None, None),
            P(ka, tau, None, None),
            P(ka),
            P(),
            P(),
            P(),
        ),
        out_specs=P(None, tau, ka, None),
        check_vma=False,
    )
```

```python
import functools

import jax
import jax.numpy as jnp
from jax import lax
from jax.experimental import pallas as pl
from jax.experimental.pallas import tpu as pltpu
from jax.sharding import Mesh
from jax.sharding import PartitionSpec as P

SIDE = 4
ROWS = 12
STEP = 4
TILE = 16
POINTS = 16
FIRST_LIMIT = 10 * 1024 * 1024
PRODUCT_LIMIT = 14 * 1024 * 1024
SMALL_LIMIT = 8 * 1024 * 1024
COST = pl.CostEstimate(flops=1000, bytes_accessed=1000, transcendentals=0)


def onehot(rows, columns):
    return (rows == columns).astype(jnp.float32).astype(jnp.bfloat16)


def swap_order(blocks):
    size = TILE * blocks
    at = lax.broadcasted_iota(jnp.int32, (size, size), 0)
    source = lax.broadcasted_iota(jnp.int32, (size, size), 1)
    return onehot(at % TILE * blocks + at // TILE, source)


def row_order(size, core):
    at = lax.broadcasted_iota(jnp.int32, (size, 1), 0)
    side = (at >= size // 2).astype(jnp.int32)
    here = core ^ side
    rest = at - side * (size // 2)
    shard = (rest * 171) >> 11
    row = rest - shard * ROWS
    outer, inner = shard >> 2, shard & 3
    y = jnp.where(here == 1, outer, inner)
    x = jnp.where(here == 1, inner, outer)
    return onehot(((y * 2 + here) * SIDE + x) * ROWS + row, lax.broadcasted_iota(jnp.int32, (size, size), 1))


def left_turn(order, piece_ref, fwd_ref, coef_ref, left_ref, turn, step):
    blocks = coef_ref.shape[0]
    width = fwd_ref.shape[-1]
    size = TILE * blocks
    pieces = [
        piece_ref[pl.ds(pl.multiple_of((turn * step + part) * size, size), size), :]
        for part in range(step)
    ]
    wide = jnp.dot(order, jnp.concatenate(pieces, axis=1), preferred_element_type=jnp.float32)
    wide = wide.astype(jnp.bfloat16)
    coefs = []
    for part in range(step):
        group = turn * step + part
        coef = wide[:, part * width : (part + 1) * width]
        spot = pl.ds(pl.multiple_of(group * TILE, TILE), TILE)
        coef_ref[:, spot, :] = coef.reshape(blocks, TILE, width)
        coefs.append(coef)
    left = jnp.dot(jnp.concatenate(coefs, axis=0), fwd_ref[...], preferred_element_type=jnp.float32)
    left = left.astype(jnp.bfloat16).reshape(step, blocks * TILE, width)
    for part in range(step):
        group = turn * step + part
        left_ref[:, pl.ds(pl.multiple_of(group * width, width), width)] = left[part]


def first_kernel(
    core_ref, piece_hbm, fwd_hbm, back_hbm, coef_ref, left_ref, fwd_ref, back_t_ref, piece_ref, back_ref, sems
):
    blocks = coef_ref.shape[0]
    order = swap_order(blocks)
    step = STEP
    turns = coef_ref.shape[1] // TILE // step
    size = step * TILE * blocks

    def piece_copy(turn):
        spot = pl.ds(pl.multiple_of(turn * size, size), size)
        return pltpu.make_async_copy(piece_hbm.at[spot], piece_ref.at[spot], sems.at[turn])

    fwd_copy = pltpu.make_async_copy(fwd_hbm, fwd_ref, sems.at[turns])
    back_copy = pltpu.make_async_copy(back_hbm, back_ref, sems.at[turns + 1])
    piece_copy(0).start()
    fwd_copy.start()
    for turn in range(1, turns):
        piece_copy(turn).start()
    back_copy.start()
    fwd_copy.wait()

    @pl.loop(0, turns)
    def _(turn):
        piece_copy(turn).wait()
        left_turn(order, piece_ref, fwd_ref, coef_ref, left_ref, turn, step)

    back_copy.wait()
    rows = row_order(back_ref.shape[0], core_ref[0])
    back = jnp.dot(rows, back_ref[...], preferred_element_type=jnp.float32).astype(jnp.bfloat16)
    back_t = lax.dot_general(
        rows, back, (((1,), (1,)), ((), ())), preferred_element_type=jnp.float32
    )
    back_t_ref[...] = back_t.astype(jnp.bfloat16)


def left_kernel(piece_ref, fwd_ref, coef_ref, left_ref):
    order = swap_order(coef_ref.shape[0])
    step = STEP

    @pl.loop(0, coef_ref.shape[1] // TILE // step)
    def _(turn):
        left_turn(order, piece_ref, fwd_ref, coef_ref, left_ref, turn, step)


def product_kernel(
    coef_mine_ref, coef_other_ref, left_mine_ref, left_other_ref, back_t_ref, out_ref, right_ref
):
    blocks, half, width = coef_mine_ref.shape
    per_side = half // TILE

    @pl.loop(0, blocks // 2, unroll=4)
    def _(pair):
        coefs = []
        for p in (2 * pair, 2 * pair + 1):
            coefs.append(jnp.concatenate([coef_mine_ref[p], coef_other_ref[p]], axis=0))
        right = jnp.dot(
            back_t_ref[...], jnp.concatenate(coefs, axis=1), preferred_element_type=jnp.float32
        )
        right = right.astype(jnp.bfloat16)
        for inner in range(2):
            rows = pl.ds(pl.multiple_of((2 * pair + inner) * TILE, TILE), TILE)
            for block in range(2 * per_side):
                at = block % per_side * width
                right_ref[block // per_side, rows, at : at + width] = right[
                    block * TILE : (block + 1) * TILE, inner * width : (inner + 1) * width
                ]

    size = TILE * blocks
    gram = jnp.zeros((size, size), jnp.float32)
    for side, lefts in enumerate((left_mine_ref, left_other_ref)):
        gram += lax.dot_general(
            lefts[...], right_ref[side], (((1,), (1,)), ((), ())), preferred_element_type=jnp.float32
        )
    row = lax.broadcasted_iota(jnp.int32, (size, size), 0) % TILE
    column = lax.broadcasted_iota(jnp.int32, (size, size), 1) % TILE
    gram = jnp.where(row == column, gram, 0.0)
    gram = jnp.sum(gram.reshape(blocks, TILE, size), axis=1)
    at = lax.broadcasted_iota(jnp.int32, (size, blocks), 0) // TILE
    which = lax.broadcasted_iota(jnp.int32, (size, blocks), 1)
    pick = (at == which).astype(jnp.float32)
    polar = jnp.dot(gram, pick, precision=lax.Precision.HIGHEST, preferred_element_type=jnp.float32)
    polar = polar * (-1.0 / POINTS)
    _, cores, _ = out_ref.shape
    for p in range(blocks):
        for copy in range(out_ref.shape[0] * cores // blocks):
            place = p // cores * (out_ref.shape[0] * cores // blocks) + copy
            out_ref[place, p % cores : p % cores + 1, :] = polar[p : p + 1, :]


def half_shapes(piece, blocks):
    width = piece.shape[-1]
    half = piece.shape[0] // blocks
    coef = jax.ShapeDtypeStruct((blocks, half, width), jnp.bfloat16)
    left = jax.ShapeDtypeStruct((blocks * TILE, half // TILE * width), jnp.bfloat16)
    return coef, left


def first_half(core, piece, green_fwd, green_back, blocks):
    width = green_fwd.shape[-1]
    square = jax.ShapeDtypeStruct((width, width), jnp.bfloat16)
    return pl.pallas_call(
        first_kernel,
        out_shape=half_shapes(piece, blocks) + (square, square),
        in_specs=[pl.BlockSpec(memory_space=pltpu.SMEM)]
        + [pl.BlockSpec(memory_space=pl.ANY)] * 3,
        out_specs=[pl.BlockSpec(memory_space=pltpu.VMEM)] * 4,
        scratch_shapes=[
            pltpu.VMEM(piece.shape, jnp.bfloat16),
            pltpu.VMEM((width, width), jnp.bfloat16),
            pltpu.SemaphoreType.DMA((piece.shape[0] // (STEP * TILE * blocks) + 2,)),
        ],
        compiler_params=pltpu.CompilerParams(vmem_limit_bytes=FIRST_LIMIT),
        cost_estimate=COST,
    )(core, piece, green_fwd, green_back)


def second_half(piece, green_fwd, blocks):
    return pl.pallas_call(
        left_kernel,
        out_shape=half_shapes(piece, blocks),
        in_specs=[pl.BlockSpec(memory_space=pltpu.VMEM)] * 2,
        out_specs=[pl.BlockSpec(memory_space=pltpu.VMEM)] * 2,
        compiler_params=pltpu.CompilerParams(vmem_limit_bytes=SMALL_LIMIT),
        cost_estimate=COST,
    )(piece, green_fwd)


def product(coef_mine, coef_other, left_mine, left_other, back_t, receivers, cores):
    blocks, half, width = coef_mine.shape
    return pl.pallas_call(
        product_kernel,
        out_shape=jax.ShapeDtypeStruct((receivers, cores, blocks), jnp.float32),
        in_specs=[pl.BlockSpec(memory_space=pltpu.VMEM)] * 5,
        out_specs=pl.BlockSpec(memory_space=pltpu.VMEM),
        scratch_shapes=[
            pltpu.VMEM((2, blocks * TILE, half // TILE * width), jnp.bfloat16),
        ],
        compiler_params=pltpu.CompilerParams(vmem_limit_bytes=PRODUCT_LIMIT),
        cost_estimate=COST,
    )(coef_mine, coef_other, left_mine, left_other, back_t)


def settle_kernel(block_ref, out_ref):
    out_ref[...] = block_ref[...]


def settled(block):
    return pl.pallas_call(
        settle_kernel,
        out_shape=jax.ShapeDtypeStruct(block.shape, block.dtype),
        in_specs=[pl.BlockSpec(memory_space=pltpu.VMEM)],
        out_specs=pl.BlockSpec(memory_space=pltpu.VMEM),
        compiler_params=pltpu.CompilerParams(vmem_limit_bytes=SMALL_LIMIT),
        cost_estimate=pl.CostEstimate(
            flops=50_000_000_000, bytes_accessed=2_500_000, transcendentals=0
        ),
    )(block)


def spread(block, phases):
    for groups in phases:
        count = len(groups[0])
        copies = jnp.broadcast_to(block[None], (count,) + block.shape)
        block = lax.all_to_all(
            copies, ("c", "y", "x"), 0, 0, axis_index_groups=groups, tiled=True
        ).reshape(count * block.shape[0], block.shape[1])
    return block


def spread_phases(cores, ys, xs):
    def index(c, y, x):
        return (c * ys + y) * xs + x

    along_y = [[[index(c, y, x) for y in range(ys)] for x in range(xs)] for c in range(cores)]
    along_x = [[[index(c, y, x) for x in range(xs)] for y in range(ys)] for c in range(cores)]
    return along_y[0] + along_x[1], along_x[0] + along_y[1]


def shards(sizes, bcoef, fwd_green, back_green, kmq, ir_table, ir_fit, freq_index):
    zl, cores, ys, zh, xs = (sizes[name] for name in ("zl", "c", "y", "zh", "x"))
    blocks, rows, orb = bcoef.shape[1:]
    points = zl * cores
    minor = points // SIDE
    core = lax.axis_index("c")
    high = lax.axis_index("zh")
    low = lax.axis_index("zl")
    here_y, here_x = lax.axis_index("y"), lax.axis_index("x")

    own_w = (here_y * zh + high) * xs + here_x
    own_k = low * cores + core
    target = kmq[0]
    major_shift = ((own_k >> 2) - (target >> 2)) & 3
    minor_shift = ((own_k & 3) - (target & 3)) & 3
    branch = (major_shift - 1) * (minor - 1) + minor_shift - 1

    phases = spread_phases(cores, ys, xs)
    swapped = [(c * zh + h, h * zh + c) for c in range(cores) for h in range(zh)]

    def partner(major, minor_by):
        route = []
        for k in range(points):
            a, b = divmod(k, minor)
            source = (a - major) % SIDE * minor + (b - minor_by) % minor
            for h in range(zh):
                route.append((source * zh + h, (k // cores * cores + h) * zh + k % cores))

        def work(shard, green_fwd, green_back):
            shard = shard.transpose(1, 0, 2).reshape(rows * blocks, orb)
            shard = lax.ppermute(shard, ("c", "zh"), swapped)
            green_fwd = lax.ppermute(green_fwd, ("c", "zh"), swapped)
            green_back = lax.ppermute(green_back, ("zl", "c", "zh"), route)
            mine = lax.cond(
                target >= 0,
                lambda block: spread(block, phases),
                lambda block: jnp.zeros((ys * xs * block.shape[0], block.shape[1]), block.dtype),
                settled(shard),
            )
            return mine, green_fwd, green_back

        return work

    works = [partner(a, b) for a in range(1, SIDE) for b in range(1, minor)]
    mine, green_fwd, green_back = lax.switch(
        branch, works, bcoef[0], fwd_green[0, 0], back_green[0, 0]
    )
    mine, own_w, core = lax.optimization_barrier((mine, own_w.astype(jnp.uint32), core))
    other = lax.ppermute(mine, "c", [(0, 1), (1, 0)])
    coef_mine, left_mine, green_fwd, back_t = first_half(
        core[None], mine, green_fwd, green_back, blocks
    )
    coef_other, left_other = second_half(other, green_fwd, blocks)
    pairs = product(coef_mine, coef_other, left_mine, left_other, back_t, zl * zh, cores)
    pairs, ir_table, ir_fit, freq_index = lax.optimization_barrier(
        (pairs, ir_table, ir_fit, freq_index)
    )
    parts = lax.all_to_all(pairs, ("zl", "zh"), 0, 0, tiled=True)
    summed = jnp.sum(parts, axis=0)
    entries = jnp.broadcast_to(summed[:, None, :], (cores, ys * xs, blocks))
    entries = entries.reshape(cores * ys * xs, blocks)
    times = lax.all_to_all(entries, ("c", "y", "x"), 0, 0, tiled=True)
    chosen = lax.dynamic_slice_in_dim(ir_table, lax.dynamic_slice(freq_index, (own_w,), (1,))[0], 1, axis=1)
    fit = ir_fit.reshape(-1, ys, cores, xs).transpose(0, 2, 1, 3).reshape(ir_fit.shape)
    transform = jnp.sum(chosen.transpose(0, 2, 1) * fit[None], axis=1)
    result = jnp.sum(transform[:, :, None] * times[None], axis=1)
    return result[:, None, None, :]


def solution(mesh):
    sizes = {"zl": 8, "c": 2, "y": 4, "zh": 2, "x": 4}
    fine = Mesh(mesh.devices.reshape(tuple(sizes.values())), tuple(sizes))
    ka, tau = ("zl", "c"), ("y", "zh", "x")
    return jax.shard_map(
        functools.partial(shards, sizes),
        mesh=fine,
        in_specs=(
            P(ka, None, tau, None),
            P(ka, tau, None, None),
            P(ka, tau, None, None),
            P(ka),
            P(),
            P(),
            P(),
        ),
        out_specs=P(None, tau, ka, None),
        check_vma=False,
    )
```

```python
import functools

import jax
import jax.numpy as jnp
from jax import lax
from jax.experimental import pallas as pl
from jax.experimental.pallas import tpu as pltpu
from jax.sharding import Mesh
from jax.sharding import PartitionSpec as P

SIDE = 4
ROWS = 12
STEP = 4
TILE = 16
POINTS = 16
FIRST_LIMIT = 10 * 1024 * 1024
PRODUCT_LIMIT = 14 * 1024 * 1024
SMALL_LIMIT = 8 * 1024 * 1024
COST = pl.CostEstimate(flops=1000, bytes_accessed=1000, transcendentals=0)


def onehot(rows, columns):
    return (rows == columns).astype(jnp.float32).astype(jnp.bfloat16)


def swap_order(blocks):
    size = TILE * blocks
    at = lax.broadcasted_iota(jnp.int32, (size, size), 0)
    source = lax.broadcasted_iota(jnp.int32, (size, size), 1)
    return onehot(at % TILE * blocks + at // TILE, source)


def row_order(size, core):
    at = lax.broadcasted_iota(jnp.int32, (size, 1), 0)
    side = (at >= size // 2).astype(jnp.int32)
    here = core ^ side
    rest = at - side * (size // 2)
    shard = (rest * 171) >> 11
    row = rest - shard * ROWS
    y, x = shard >> 2, shard & 3
    return onehot(((y * 2 + here) * SIDE + x) * ROWS + row, lax.broadcasted_iota(jnp.int32, (size, size), 1))


def left_turn(order, piece_ref, fwd_ref, coef_ref, left_ref, turn, step):
    blocks = coef_ref.shape[0]
    width = fwd_ref.shape[-1]
    size = TILE * blocks
    pieces = [
        piece_ref[pl.ds(pl.multiple_of((turn * step + part) * size, size), size), :]
        for part in range(step)
    ]
    wide = jnp.dot(order, jnp.concatenate(pieces, axis=1), preferred_element_type=jnp.float32)
    wide = wide.astype(jnp.bfloat16)
    coefs = []
    for part in range(step):
        group = turn * step + part
        coef = wide[:, part * width : (part + 1) * width]
        spot = pl.ds(pl.multiple_of(group * TILE, TILE), TILE)
        coef_ref[:, spot, :] = coef.reshape(blocks, TILE, width)
        coefs.append(coef)
    left = jnp.dot(jnp.concatenate(coefs, axis=0), fwd_ref[...], preferred_element_type=jnp.float32)
    left = left.astype(jnp.bfloat16).reshape(step, blocks * TILE, width)
    for part in range(step):
        group = turn * step + part
        left_ref[:, pl.ds(pl.multiple_of(group * width, width), width)] = left[part]


def first_kernel(
    core_ref, piece_hbm, fwd_hbm, back_hbm, coef_ref, left_ref, fwd_ref, back_t_ref, piece_ref, back_ref, sems
):
    blocks = coef_ref.shape[0]
    order = swap_order(blocks)
    step = STEP
    turns = coef_ref.shape[1] // TILE // step
    size = step * TILE * blocks

    def piece_copy(turn):
        spot = pl.ds(pl.multiple_of(turn * size, size), size)
        return pltpu.make_async_copy(piece_hbm.at[spot], piece_ref.at[spot], sems.at[turn])

    fwd_copy = pltpu.make_async_copy(fwd_hbm, fwd_ref, sems.at[turns])
    back_copy = pltpu.make_async_copy(back_hbm, back_ref, sems.at[turns + 1])
    piece_copy(0).start()
    fwd_copy.start()
    for turn in range(1, turns):
        piece_copy(turn).start()
    back_copy.start()
    fwd_copy.wait()

    @pl.loop(0, turns)
    def _(turn):
        piece_copy(turn).wait()
        left_turn(order, piece_ref, fwd_ref, coef_ref, left_ref, turn, step)

    back_copy.wait()
    rows = row_order(back_ref.shape[0], core_ref[0])
    back = jnp.dot(rows, back_ref[...], preferred_element_type=jnp.float32).astype(jnp.bfloat16)
    back_t = lax.dot_general(
        rows, back, (((1,), (1,)), ((), ())), preferred_element_type=jnp.float32
    )
    back_t_ref[...] = back_t.astype(jnp.bfloat16)


def left_kernel(piece_ref, fwd_ref, coef_ref, left_ref):
    order = swap_order(coef_ref.shape[0])
    step = STEP

    @pl.loop(0, coef_ref.shape[1] // TILE // step)
    def _(turn):
        left_turn(order, piece_ref, fwd_ref, coef_ref, left_ref, turn, step)


def product_kernel(
    coef_mine_ref, coef_other_ref, left_mine_ref, left_other_ref, back_t_ref, out_ref, right_ref
):
    blocks, half, width = coef_mine_ref.shape
    per_side = half // TILE

    @pl.loop(0, blocks // 2, unroll=4)
    def _(pair):
        coefs = []
        for p in (2 * pair, 2 * pair + 1):
            coefs.append(jnp.concatenate([coef_mine_ref[p], coef_other_ref[p]], axis=0))
        right = jnp.dot(
            back_t_ref[...], jnp.concatenate(coefs, axis=1), preferred_element_type=jnp.float32
        )
        right = right.astype(jnp.bfloat16)
        for inner in range(2):
            rows = pl.ds(pl.multiple_of((2 * pair + inner) * TILE, TILE), TILE)
            for block in range(2 * per_side):
                at = block % per_side * width
                right_ref[block // per_side, rows, at : at + width] = right[
                    block * TILE : (block + 1) * TILE, inner * width : (inner + 1) * width
                ]

    size = TILE * blocks
    gram = jnp.zeros((size, size), jnp.float32)
    for side, lefts in enumerate((left_mine_ref, left_other_ref)):
        gram += lax.dot_general(
            lefts[...], right_ref[side], (((1,), (1,)), ((), ())), preferred_element_type=jnp.float32
        )
    row = lax.broadcasted_iota(jnp.int32, (size, size), 0) % TILE
    column = lax.broadcasted_iota(jnp.int32, (size, size), 1) % TILE
    gram = jnp.where(row == column, gram, 0.0)
    gram = jnp.sum(gram.reshape(blocks, TILE, size), axis=1)
    at = lax.broadcasted_iota(jnp.int32, (size, blocks), 0) // TILE
    which = lax.broadcasted_iota(jnp.int32, (size, blocks), 1)
    pick = (at == which).astype(jnp.float32)
    polar = jnp.dot(gram, pick, precision=lax.Precision.HIGHEST, preferred_element_type=jnp.float32)
    polar = polar * (-1.0 / POINTS)
    _, cores, _ = out_ref.shape
    for p in range(blocks):
        for copy in range(out_ref.shape[0] * cores // blocks):
            place = p // cores * (out_ref.shape[0] * cores // blocks) + copy
            out_ref[place, p % cores : p % cores + 1, :] = polar[p : p + 1, :]


def half_shapes(piece, blocks):
    width = piece.shape[-1]
    half = piece.shape[0] // blocks
    coef = jax.ShapeDtypeStruct((blocks, half, width), jnp.bfloat16)
    left = jax.ShapeDtypeStruct((blocks * TILE, half // TILE * width), jnp.bfloat16)
    return coef, left


def first_half(core, piece, green_fwd, green_back, blocks):
    width = green_fwd.shape[-1]
    square = jax.ShapeDtypeStruct((width, width), jnp.bfloat16)
    return pl.pallas_call(
        first_kernel,
        out_shape=half_shapes(piece, blocks) + (square, square),
        in_specs=[pl.BlockSpec(memory_space=pltpu.SMEM)]
        + [pl.BlockSpec(memory_space=pl.ANY)] * 3,
        out_specs=[pl.BlockSpec(memory_space=pltpu.VMEM)] * 4,
        scratch_shapes=[
            pltpu.VMEM(piece.shape, jnp.bfloat16),
            pltpu.VMEM((width, width), jnp.bfloat16),
            pltpu.SemaphoreType.DMA((piece.shape[0] // (STEP * TILE * blocks) + 2,)),
        ],
        compiler_params=pltpu.CompilerParams(vmem_limit_bytes=FIRST_LIMIT),
        cost_estimate=COST,
    )(core, piece, green_fwd, green_back)


def second_half(piece, green_fwd, blocks):
    return pl.pallas_call(
        left_kernel,
        out_shape=half_shapes(piece, blocks),
        in_specs=[pl.BlockSpec(memory_space=pltpu.VMEM)] * 2,
        out_specs=[pl.BlockSpec(memory_space=pltpu.VMEM)] * 2,
        compiler_params=pltpu.CompilerParams(vmem_limit_bytes=SMALL_LIMIT),
        cost_estimate=COST,
    )(piece, green_fwd)


def product(coef_mine, coef_other, left_mine, left_other, back_t, receivers, cores):
    blocks, half, width = coef_mine.shape
    return pl.pallas_call(
        product_kernel,
        out_shape=jax.ShapeDtypeStruct((receivers, cores, blocks), jnp.float32),
        in_specs=[pl.BlockSpec(memory_space=pltpu.VMEM)] * 5,
        out_specs=pl.BlockSpec(memory_space=pltpu.VMEM),
        scratch_shapes=[
            pltpu.VMEM((2, blocks * TILE, half // TILE * width), jnp.bfloat16),
        ],
        compiler_params=pltpu.CompilerParams(vmem_limit_bytes=PRODUCT_LIMIT),
        cost_estimate=COST,
    )(coef_mine, coef_other, left_mine, left_other, back_t)


def settle_kernel(block_ref, out_ref):
    out_ref[...] = block_ref[...]


def settled(block):
    return pl.pallas_call(
        settle_kernel,
        out_shape=jax.ShapeDtypeStruct(block.shape, block.dtype),
        in_specs=[pl.BlockSpec(memory_space=pltpu.VMEM)],
        out_specs=pl.BlockSpec(memory_space=pltpu.VMEM),
        compiler_params=pltpu.CompilerParams(vmem_limit_bytes=SMALL_LIMIT),
        cost_estimate=pl.CostEstimate(
            flops=50_000_000_000, bytes_accessed=2_500_000, transcendentals=0
        ),
    )(block)


def spread(block, axes, count):
    copies = jnp.broadcast_to(block[None], (count,) + block.shape)
    rows = lax.all_to_all(copies, axes, 0, 0, tiled=True)
    return rows.reshape(count * block.shape[0], block.shape[1])


def shards(sizes, bcoef, fwd_green, back_green, kmq, ir_table, ir_fit, freq_index):
    zl, cores, ys, zh, xs = (sizes[name] for name in ("zl", "c", "y", "zh", "x"))
    blocks, rows, orb = bcoef.shape[1:]
    points = zl * cores
    minor = points // SIDE
    core = lax.axis_index("c")
    high = lax.axis_index("zh")
    low = lax.axis_index("zl")
    here_y, here_x = lax.axis_index("y"), lax.axis_index("x")

    own_w = (here_y * zh + high) * xs + here_x
    own_k = low * cores + core
    target = kmq[0]
    major_shift = ((own_k >> 2) - (target >> 2)) & 3
    minor_shift = ((own_k & 3) - (target & 3)) & 3
    branch = (major_shift - 1) * (minor - 1) + minor_shift - 1

    swapped = [(c * zh + h, h * zh + c) for c in range(cores) for h in range(zh)]

    def partner(major, minor_by):
        route = []
        for k in range(points):
            a, b = divmod(k, minor)
            source = (a - major) % SIDE * minor + (b - minor_by) % minor
            for h in range(zh):
                route.append((source * zh + h, (k // cores * cores + h) * zh + k % cores))

        def work(shard, green_fwd, green_back):
            shard = shard.transpose(1, 0, 2).reshape(rows * blocks, orb)
            shard = lax.ppermute(shard, ("c", "zh"), swapped)
            green_fwd = lax.ppermute(green_fwd, ("c", "zh"), swapped)
            green_back = lax.ppermute(green_back, ("zl", "c", "zh"), route)
            mine = lax.cond(
                target >= 0,
                lambda block: spread(block, ("y", "x"), ys * xs),
                lambda block: jnp.zeros((ys * xs * block.shape[0], block.shape[1]), block.dtype),
                settled(shard),
            )
            return mine, green_fwd, green_back

        return work

    works = [partner(a, b) for a in range(1, SIDE) for b in range(1, minor)]
    mine, green_fwd, green_back = lax.switch(
        branch, works, bcoef[0], fwd_green[0, 0], back_green[0, 0]
    )
    mine, own_w, core = lax.optimization_barrier((mine, own_w.astype(jnp.uint32), core))
    other = lax.ppermute(mine, "c", [(0, 1), (1, 0)])
    coef_mine, left_mine, green_fwd, back_t = first_half(
        core[None], mine, green_fwd, green_back, blocks
    )
    coef_other, left_other = second_half(other, green_fwd, blocks)
    pairs = product(coef_mine, coef_other, left_mine, left_other, back_t, zl * zh, cores)
    pairs, ir_table, ir_fit, freq_index = lax.optimization_barrier(
        (pairs, ir_table, ir_fit, freq_index)
    )
    parts = lax.all_to_all(pairs, ("zl", "zh"), 0, 0, tiled=True)
    summed = jnp.sum(parts, axis=0)
    entries = jnp.broadcast_to(summed[:, None, :], (cores, ys * xs, blocks))
    entries = entries.reshape(cores * ys * xs, blocks)
    times = lax.all_to_all(entries, ("c", "y", "x"), 0, 0, tiled=True)
    chosen = lax.dynamic_slice_in_dim(ir_table, lax.dynamic_slice(freq_index, (own_w,), (1,))[0], 1, axis=1)
    fit = ir_fit.reshape(-1, ys, cores, xs).transpose(0, 2, 1, 3).reshape(ir_fit.shape)
    transform = jnp.sum(chosen.transpose(0, 2, 1) * fit[None], axis=1)
    result = jnp.sum(transform[:, :, None] * times[None], axis=1)
    return result[:, None, None, :]


def solution(mesh):
    sizes = {"zl": 8, "c": 2, "y": 4, "zh": 2, "x": 4}
    fine = Mesh(mesh.devices.reshape(tuple(sizes.values())), tuple(sizes))
    ka, tau = ("zl", "c"), ("y", "zh", "x")
    return jax.shard_map(
        functools.partial(shards, sizes),
        mesh=fine,
        in_specs=(
            P(ka, None, tau, None),
            P(ka, tau, None, None),
            P(ka, tau, None, None),
            P(ka),
            P(),
            P(),
            P(),
        ),
        out_specs=P(None, tau, ka, None),
        check_vma=False,
    )
```

```python
import functools

import jax
import jax.numpy as jnp
from jax import lax
from jax.experimental import pallas as pl
from jax.experimental.pallas import tpu as pltpu
from jax.sharding import Mesh
from jax.sharding import PartitionSpec as P

SIDE = 4
ROWS = 12
STEP = 4
TILE = 16
POINTS = 16
FIRST_LIMIT = 10 * 1024 * 1024
PRODUCT_LIMIT = 14 * 1024 * 1024
SMALL_LIMIT = 8 * 1024 * 1024
COST = pl.CostEstimate(flops=1000, bytes_accessed=1000, transcendentals=0)


def onehot(rows, columns):
    return (rows == columns).astype(jnp.float32).astype(jnp.bfloat16)


def swap_order(blocks):
    size = TILE * blocks
    at = lax.broadcasted_iota(jnp.int32, (size, size), 0)
    source = lax.broadcasted_iota(jnp.int32, (size, size), 1)
    return onehot(at % TILE * blocks + at // TILE, source)


def row_order(size, core):
    at = lax.broadcasted_iota(jnp.int32, (size, 1), 0)
    side = (at >= size // 2).astype(jnp.int32)
    here = core ^ side
    rest = at - side * (size // 2)
    shard = (rest * 171) >> 11
    row = rest - shard * ROWS
    y, x = shard >> 2, shard & 3
    return onehot(((y * 2 + here) * SIDE + x) * ROWS + row, lax.broadcasted_iota(jnp.int32, (size, size), 1))


def left_turn(order, piece_ref, fwd_ref, coef_ref, left_ref, turn, step):
    blocks = coef_ref.shape[0]
    width = fwd_ref.shape[-1]
    size = TILE * blocks
    pieces = [
        piece_ref[pl.ds(pl.multiple_of((turn * step + part) * size, size), size), :]
        for part in range(step)
    ]
    wide = jnp.dot(order, jnp.concatenate(pieces, axis=1), preferred_element_type=jnp.float32)
    wide = wide.astype(jnp.bfloat16)
    coefs = []
    for part in range(step):
        group = turn * step + part
        coef = wide[:, part * width : (part + 1) * width]
        spot = pl.ds(pl.multiple_of(group * TILE, TILE), TILE)
        coef_ref[:, spot, :] = coef.reshape(blocks, TILE, width)
        coefs.append(coef)
    left = jnp.dot(jnp.concatenate(coefs, axis=0), fwd_ref[...], preferred_element_type=jnp.float32)
    left = left.astype(jnp.bfloat16).reshape(step, blocks * TILE, width)
    for part in range(step):
        group = turn * step + part
        left_ref[:, pl.ds(pl.multiple_of(group * width, width), width)] = left[part]


def first_kernel(
    core_ref, piece_hbm, fwd_hbm, back_hbm, coef_ref, left_ref, fwd_ref, back_t_ref, piece_ref, back_ref, sems
):
    blocks = coef_ref.shape[0]
    order = swap_order(blocks)
    step = STEP
    turns = coef_ref.shape[1] // TILE // step
    size = step * TILE * blocks

    def piece_copy(turn):
        spot = pl.ds(pl.multiple_of(turn * size, size), size)
        return pltpu.make_async_copy(piece_hbm.at[spot], piece_ref.at[spot], sems.at[turn])

    fwd_copy = pltpu.make_async_copy(fwd_hbm, fwd_ref, sems.at[turns])
    back_copy = pltpu.make_async_copy(back_hbm, back_ref, sems.at[turns + 1])
    piece_copy(0).start()
    fwd_copy.start()
    for turn in range(1, turns):
        piece_copy(turn).start()
    back_copy.start()
    fwd_copy.wait()

    @pl.loop(0, turns)
    def _(turn):
        piece_copy(turn).wait()
        left_turn(order, piece_ref, fwd_ref, coef_ref, left_ref, turn, step)

    back_copy.wait()
    rows = row_order(back_ref.shape[0], core_ref[0])
    back = jnp.dot(rows, back_ref[...], preferred_element_type=jnp.float32).astype(jnp.bfloat16)
    back_t = lax.dot_general(
        rows, back, (((1,), (1,)), ((), ())), preferred_element_type=jnp.float32
    )
    back_t_ref[...] = back_t.astype(jnp.bfloat16)


def left_kernel(piece_ref, fwd_ref, coef_ref, left_ref):
    order = swap_order(coef_ref.shape[0])
    step = STEP

    @pl.loop(0, coef_ref.shape[1] // TILE // step)
    def _(turn):
        left_turn(order, piece_ref, fwd_ref, coef_ref, left_ref, turn, step)


def product_kernel(
    coef_mine_ref, coef_other_ref, left_mine_ref, left_other_ref, back_t_ref, out_ref, right_ref
):
    blocks, half, width = coef_mine_ref.shape
    per_side = half // TILE

    @pl.loop(0, blocks // 2, unroll=4)
    def _(pair):
        coefs = []
        for p in (2 * pair, 2 * pair + 1):
            coefs.append(jnp.concatenate([coef_mine_ref[p], coef_other_ref[p]], axis=0))
        right = jnp.dot(
            back_t_ref[...], jnp.concatenate(coefs, axis=1), preferred_element_type=jnp.float32
        )
        right = right.astype(jnp.bfloat16)
        for inner in range(2):
            rows = pl.ds(pl.multiple_of((2 * pair + inner) * TILE, TILE), TILE)
            for block in range(2 * per_side):
                at = block % per_side * width
                right_ref[block // per_side, rows, at : at + width] = right[
                    block * TILE : (block + 1) * TILE, inner * width : (inner + 1) * width
                ]

    size = TILE * blocks
    gram = jnp.zeros((size, size), jnp.float32)
    for side, lefts in enumerate((left_mine_ref, left_other_ref)):
        gram += lax.dot_general(
            lefts[...], right_ref[side], (((1,), (1,)), ((), ())), preferred_element_type=jnp.float32
        )
    row = lax.broadcasted_iota(jnp.int32, (size, size), 0) % TILE
    column = lax.broadcasted_iota(jnp.int32, (size, size), 1) % TILE
    gram = jnp.where(row == column, gram, 0.0)
    gram = jnp.sum(gram.reshape(blocks, TILE, size), axis=1)
    at = lax.broadcasted_iota(jnp.int32, (size, blocks), 0) // TILE
    which = lax.broadcasted_iota(jnp.int32, (size, blocks), 1)
    pick = (at == which).astype(jnp.float32)
    polar = jnp.dot(gram, pick, precision=lax.Precision.HIGHEST, preferred_element_type=jnp.float32)
    polar = polar * (-1.0 / POINTS)
    _, cores, _ = out_ref.shape
    for p in range(blocks):
        for copy in range(out_ref.shape[0] * cores // blocks):
            place = p // cores * (out_ref.shape[0] * cores // blocks) + copy
            out_ref[place, p % cores : p % cores + 1, :] = polar[p : p + 1, :]


def half_shapes(piece, blocks):
    width = piece.shape[-1]
    half = piece.shape[0] // blocks
    coef = jax.ShapeDtypeStruct((blocks, half, width), jnp.bfloat16)
    left = jax.ShapeDtypeStruct((blocks * TILE, half // TILE * width), jnp.bfloat16)
    return coef, left


def first_half(core, piece, green_fwd, green_back, blocks):
    width = green_fwd.shape[-1]
    square = jax.ShapeDtypeStruct((width, width), jnp.bfloat16)
    return pl.pallas_call(
        first_kernel,
        out_shape=half_shapes(piece, blocks) + (square, square),
        in_specs=[pl.BlockSpec(memory_space=pltpu.SMEM)]
        + [pl.BlockSpec(memory_space=pl.ANY)] * 3,
        out_specs=[pl.BlockSpec(memory_space=pltpu.VMEM)] * 4,
        scratch_shapes=[
            pltpu.VMEM(piece.shape, jnp.bfloat16),
            pltpu.VMEM((width, width), jnp.bfloat16),
            pltpu.SemaphoreType.DMA((piece.shape[0] // (STEP * TILE * blocks) + 2,)),
        ],
        compiler_params=pltpu.CompilerParams(vmem_limit_bytes=FIRST_LIMIT),
        cost_estimate=COST,
    )(core, piece, green_fwd, green_back)


def second_half(piece, green_fwd, blocks):
    return pl.pallas_call(
        left_kernel,
        out_shape=half_shapes(piece, blocks),
        in_specs=[pl.BlockSpec(memory_space=pltpu.VMEM)] * 2,
        out_specs=[pl.BlockSpec(memory_space=pltpu.VMEM)] * 2,
        compiler_params=pltpu.CompilerParams(vmem_limit_bytes=SMALL_LIMIT),
        cost_estimate=COST,
    )(piece, green_fwd)


def product(coef_mine, coef_other, left_mine, left_other, back_t, receivers, cores):
    blocks, half, width = coef_mine.shape
    return pl.pallas_call(
        product_kernel,
        out_shape=jax.ShapeDtypeStruct((receivers, cores, blocks), jnp.float32),
        in_specs=[pl.BlockSpec(memory_space=pltpu.VMEM)] * 5,
        out_specs=pl.BlockSpec(memory_space=pltpu.VMEM),
        scratch_shapes=[
            pltpu.VMEM((2, blocks * TILE, half // TILE * width), jnp.bfloat16),
        ],
        compiler_params=pltpu.CompilerParams(vmem_limit_bytes=PRODUCT_LIMIT),
        cost_estimate=COST,
    )(coef_mine, coef_other, left_mine, left_other, back_t)


def settle_kernel(block_ref, out_ref):
    out_ref[...] = block_ref[...]


def settled(block):
    return pl.pallas_call(
        settle_kernel,
        out_shape=jax.ShapeDtypeStruct(block.shape, block.dtype),
        in_specs=[pl.BlockSpec(memory_space=pltpu.VMEM)],
        out_specs=pl.BlockSpec(memory_space=pltpu.VMEM),
        compiler_params=pltpu.CompilerParams(vmem_limit_bytes=SMALL_LIMIT),
        cost_estimate=pl.CostEstimate(
            flops=50_000_000_000, bytes_accessed=2_500_000, transcendentals=0
        ),
    )(block)


def spread(block, axes, count):
    copies = jnp.broadcast_to(block[None], (count,) + block.shape)
    rows = lax.all_to_all(copies, axes, 0, 0, tiled=True)
    return rows.reshape(count * block.shape[0], block.shape[1])


def shards(sizes, bcoef, fwd_green, back_green, kmq, ir_table, ir_fit, freq_index):
    zl, cores, ys, zh, xs = (sizes[name] for name in ("zl", "c", "y", "zh", "x"))
    blocks, rows, orb = bcoef.shape[1:]
    points = zl * cores
    minor = points // SIDE
    core = lax.axis_index("c")
    high = lax.axis_index("zh")
    low = lax.axis_index("zl")
    here_y, here_x = lax.axis_index("y"), lax.axis_index("x")

    own_w = (here_y * zh + high) * xs + here_x
    own_k = low * cores + core
    target = kmq[0]
    major_shift = ((own_k >> 2) - (target >> 2)) & 3
    minor_shift = ((own_k & 3) - (target & 3)) & 3
    branch = (major_shift - 1) * (minor - 1) + minor_shift - 1

    swapped = [(c * zh + h, h * zh + c) for c in range(cores) for h in range(zh)]

    def partner(major, minor_by):
        route = []
        for k in range(points):
            a, b = divmod(k, minor)
            source = (a - major) % SIDE * minor + (b - minor_by) % minor
            for h in range(zh):
                route.append((source * zh + h, (k // cores * cores + h) * zh + k % cores))

        def work(shard, green_fwd, green_back):
            shard = shard.transpose(1, 0, 2).reshape(rows * blocks, orb)
            shard = lax.ppermute(shard, ("c", "zh"), swapped)
            green_back = lax.ppermute(green_back, ("zl", "c", "zh"), route)
            green_fwd = lax.ppermute(green_fwd, ("c", "zh"), swapped)
            mine = lax.cond(
                target >= 0,
                lambda block: spread(block, ("y", "x"), ys * xs),
                lambda block: jnp.zeros((ys * xs * block.shape[0], block.shape[1]), block.dtype),
                settled(shard),
            )
            return mine, green_back, green_fwd

        return work

    works = [partner(a, b) for a in range(1, SIDE) for b in range(1, minor)]
    mine, green_back, green_fwd = lax.switch(
        branch, works, bcoef[0], fwd_green[0, 0], back_green[0, 0]
    )
    mine, own_w, core = lax.optimization_barrier((mine, own_w.astype(jnp.uint32), core))
    other = lax.ppermute(mine, "c", [(0, 1), (1, 0)])
    coef_mine, left_mine, green_fwd, back_t = first_half(
        core[None], mine, green_fwd, green_back, blocks
    )
    coef_other, left_other = second_half(other, green_fwd, blocks)
    pairs = product(coef_mine, coef_other, left_mine, left_other, back_t, zl * zh, cores)
    pairs, ir_table, ir_fit, freq_index = lax.optimization_barrier(
        (pairs, ir_table, ir_fit, freq_index)
    )
    parts = lax.all_to_all(pairs, ("zl", "zh"), 0, 0, tiled=True)
    summed = jnp.sum(parts, axis=0)
    entries = jnp.broadcast_to(summed[:, None, :], (cores, ys * xs, blocks))
    entries = entries.reshape(cores * ys * xs, blocks)
    times = lax.all_to_all(entries, ("c", "y", "x"), 0, 0, tiled=True)
    chosen = lax.dynamic_slice_in_dim(ir_table, lax.dynamic_slice(freq_index, (own_w,), (1,))[0], 1, axis=1)
    fit = ir_fit.reshape(-1, ys, cores, xs).transpose(0, 2, 1, 3).reshape(ir_fit.shape)
    transform = jnp.sum(chosen.transpose(0, 2, 1) * fit[None], axis=1)
    result = jnp.sum(transform[:, :, None] * times[None], axis=1)
    return result[:, None, None, :]


def solution(mesh):
    sizes = {"zl": 8, "c": 2, "y": 4, "zh": 2, "x": 4}
    fine = Mesh(mesh.devices.reshape(tuple(sizes.values())), tuple(sizes))
    ka, tau = ("zl", "c"), ("y", "zh", "x")
    return jax.shard_map(
        functools.partial(shards, sizes),
        mesh=fine,
        in_specs=(
            P(ka, None, tau, None),
            P(ka, tau, None, None),
            P(ka, tau, None, None),
            P(ka),
            P(),
            P(),
            P(),
        ),
        out_specs=P(None, tau, ka, None),
        check_vma=False,
    )
```

```python
import functools

import jax
import jax.numpy as jnp
from jax import lax
from jax.experimental import pallas as pl
from jax.experimental.pallas import tpu as pltpu
from jax.sharding import Mesh
from jax.sharding import PartitionSpec as P

SIDE = 4
ROWS = 12
STEP = 4
TILE = 16
POINTS = 16
FIRST_LIMIT = 10 * 1024 * 1024
PRODUCT_LIMIT = 20 * 1024 * 1024
SMALL_LIMIT = 8 * 1024 * 1024
COST = pl.CostEstimate(flops=1000, bytes_accessed=1000, transcendentals=0)


def onehot(rows, columns):
    return (rows == columns).astype(jnp.float32).astype(jnp.bfloat16)


def swap_order(blocks):
    size = TILE * blocks
    at = lax.broadcasted_iota(jnp.int32, (size, size), 0)
    source = lax.broadcasted_iota(jnp.int32, (size, size), 1)
    return onehot(at % TILE * blocks + at // TILE, source)


def row_order(size, core):
    at = lax.broadcasted_iota(jnp.int32, (size, 1), 0)
    side = (at >= size // 2).astype(jnp.int32)
    here = core ^ side
    rest = at - side * (size // 2)
    shard = (rest * 171) >> 11
    row = rest - shard * ROWS
    y, x = shard >> 2, shard & 3
    return onehot(((y * 2 + here) * SIDE + x) * ROWS + row, lax.broadcasted_iota(jnp.int32, (size, size), 1))


def left_turn(order, piece_ref, fwd_ref, coef_ref, left_ref, turn, step):
    blocks = coef_ref.shape[0]
    width = fwd_ref.shape[-1]
    size = TILE * blocks
    pieces = [
        piece_ref[pl.ds(pl.multiple_of((turn * step + part) * size, size), size), :]
        for part in range(step)
    ]
    wide = jnp.dot(order, jnp.concatenate(pieces, axis=1), preferred_element_type=jnp.float32)
    wide = wide.astype(jnp.bfloat16)
    coefs = []
    for part in range(step):
        group = turn * step + part
        coef = wide[:, part * width : (part + 1) * width]
        spot = pl.ds(pl.multiple_of(group * TILE, TILE), TILE)
        coef_ref[:, spot, :] = coef.reshape(blocks, TILE, width)
        coefs.append(coef)
    left = jnp.dot(jnp.concatenate(coefs, axis=0), fwd_ref[...], preferred_element_type=jnp.float32)
    left = left.astype(jnp.bfloat16).reshape(step, blocks * TILE, width)
    for part in range(step):
        group = turn * step + part
        left_ref[:, pl.ds(pl.multiple_of(group * width, width), width)] = left[part]


def first_kernel(
    core_ref, piece_hbm, fwd_hbm, back_hbm, coef_ref, left_ref, fwd_ref, back_t_ref, piece_ref, back_ref, sems
):
    blocks = coef_ref.shape[0]
    order = swap_order(blocks)
    step = STEP
    turns = coef_ref.shape[1] // TILE // step
    size = step * TILE * blocks

    def piece_copy(turn):
        spot = pl.ds(pl.multiple_of(turn * size, size), size)
        return pltpu.make_async_copy(piece_hbm.at[spot], piece_ref.at[spot], sems.at[turn])

    fwd_copy = pltpu.make_async_copy(fwd_hbm, fwd_ref, sems.at[turns])
    back_copy = pltpu.make_async_copy(back_hbm, back_ref, sems.at[turns + 1])
    piece_copy(0).start()
    fwd_copy.start()
    for turn in range(1, turns):
        piece_copy(turn).start()
    back_copy.start()
    fwd_copy.wait()

    @pl.loop(0, turns)
    def _(turn):
        piece_copy(turn).wait()
        left_turn(order, piece_ref, fwd_ref, coef_ref, left_ref, turn, step)

    back_copy.wait()
    rows = row_order(back_ref.shape[0], core_ref[0])
    back = jnp.dot(rows, back_ref[...], preferred_element_type=jnp.float32).astype(jnp.bfloat16)
    back_t = lax.dot_general(
        rows, back, (((1,), (1,)), ((), ())), preferred_element_type=jnp.float32
    )
    back_t_ref[...] = back_t.astype(jnp.bfloat16)


def product_kernel(
    coef_mine_ref, left_mine_ref, piece_ref, fwd_ref, back_t_ref, out_ref, coef_other_ref, left_other_ref, right_ref
):
    blocks, half, width = coef_mine_ref.shape
    order = swap_order(blocks)

    @pl.loop(0, half // TILE // STEP)
    def _(turn):
        left_turn(order, piece_ref, fwd_ref, coef_other_ref, left_other_ref, turn, STEP)

    per_side = half // TILE

    @pl.loop(0, blocks // 2, unroll=4)
    def _(pair):
        coefs = []
        for p in (2 * pair, 2 * pair + 1):
            coefs.append(jnp.concatenate([coef_mine_ref[p], coef_other_ref[p]], axis=0))
        right = jnp.dot(
            back_t_ref[...], jnp.concatenate(coefs, axis=1), preferred_element_type=jnp.float32
        )
        right = right.astype(jnp.bfloat16)
        for inner in range(2):
            rows = pl.ds(pl.multiple_of((2 * pair + inner) * TILE, TILE), TILE)
            for block in range(2 * per_side):
                at = block % per_side * width
                right_ref[block // per_side, rows, at : at + width] = right[
                    block * TILE : (block + 1) * TILE, inner * width : (inner + 1) * width
                ]

    size = TILE * blocks
    gram = jnp.zeros((size, size), jnp.float32)
    for side, lefts in enumerate((left_mine_ref, left_other_ref)):
        gram += lax.dot_general(
            lefts[...], right_ref[side], (((1,), (1,)), ((), ())), preferred_element_type=jnp.float32
        )
    row = lax.broadcasted_iota(jnp.int32, (size, size), 0) % TILE
    column = lax.broadcasted_iota(jnp.int32, (size, size), 1) % TILE
    gram = jnp.where(row == column, gram, 0.0)
    gram = jnp.sum(gram.reshape(blocks, TILE, size), axis=1)
    at = lax.broadcasted_iota(jnp.int32, (size, blocks), 0) // TILE
    which = lax.broadcasted_iota(jnp.int32, (size, blocks), 1)
    pick = (at == which).astype(jnp.float32)
    polar = jnp.dot(gram, pick, precision=lax.Precision.HIGHEST, preferred_element_type=jnp.float32)
    polar = polar * (-1.0 / POINTS)
    _, cores, _ = out_ref.shape
    for p in range(blocks):
        for copy in range(out_ref.shape[0] * cores // blocks):
            place = p // cores * (out_ref.shape[0] * cores // blocks) + copy
            out_ref[place, p % cores : p % cores + 1, :] = polar[p : p + 1, :]


def half_shapes(piece, blocks):
    width = piece.shape[-1]
    half = piece.shape[0] // blocks
    coef = jax.ShapeDtypeStruct((blocks, half, width), jnp.bfloat16)
    left = jax.ShapeDtypeStruct((blocks * TILE, half // TILE * width), jnp.bfloat16)
    return coef, left


def first_half(core, piece, green_fwd, green_back, blocks):
    width = green_fwd.shape[-1]
    square = jax.ShapeDtypeStruct((width, width), jnp.bfloat16)
    return pl.pallas_call(
        first_kernel,
        out_shape=half_shapes(piece, blocks) + (square, square),
        in_specs=[pl.BlockSpec(memory_space=pltpu.SMEM)]
        + [pl.BlockSpec(memory_space=pl.ANY)] * 3,
        out_specs=[pl.BlockSpec(memory_space=pltpu.VMEM)] * 4,
        scratch_shapes=[
            pltpu.VMEM(piece.shape, jnp.bfloat16),
            pltpu.VMEM((width, width), jnp.bfloat16),
            pltpu.SemaphoreType.DMA((piece.shape[0] // (STEP * TILE * blocks) + 2,)),
        ],
        compiler_params=pltpu.CompilerParams(vmem_limit_bytes=FIRST_LIMIT),
        cost_estimate=COST,
    )(core, piece, green_fwd, green_back)


def product(coef_mine, left_mine, other, green_fwd, back_t, receivers, cores):
    blocks, half, width = coef_mine.shape
    return pl.pallas_call(
        product_kernel,
        out_shape=jax.ShapeDtypeStruct((receivers, cores, blocks), jnp.float32),
        in_specs=[pl.BlockSpec(memory_space=pltpu.VMEM)] * 5,
        out_specs=pl.BlockSpec(memory_space=pltpu.VMEM),
        scratch_shapes=[
            pltpu.VMEM(coef_mine.shape, jnp.bfloat16),
            pltpu.VMEM(left_mine.shape, jnp.bfloat16),
            pltpu.VMEM((2, blocks * TILE, half // TILE * width), jnp.bfloat16),
        ],
        compiler_params=pltpu.CompilerParams(vmem_limit_bytes=PRODUCT_LIMIT),
        cost_estimate=COST,
    )(coef_mine, left_mine, other, green_fwd, back_t)


def settle_kernel(block_ref, out_ref):
    out_ref[...] = block_ref[...]


def settled(block):
    return pl.pallas_call(
        settle_kernel,
        out_shape=jax.ShapeDtypeStruct(block.shape, block.dtype),
        in_specs=[pl.BlockSpec(memory_space=pltpu.VMEM)],
        out_specs=pl.BlockSpec(memory_space=pltpu.VMEM),
        compiler_params=pltpu.CompilerParams(vmem_limit_bytes=SMALL_LIMIT),
        cost_estimate=pl.CostEstimate(
            flops=50_000_000_000, bytes_accessed=2_500_000, transcendentals=0
        ),
    )(block)


def spread(block, axes, count):
    copies = jnp.broadcast_to(block[None], (count,) + block.shape)
    rows = lax.all_to_all(copies, axes, 0, 0, tiled=True)
    return rows.reshape(count * block.shape[0], block.shape[1])


def shards(sizes, bcoef, fwd_green, back_green, kmq, ir_table, ir_fit, freq_index):
    zl, cores, ys, zh, xs = (sizes[name] for name in ("zl", "c", "y", "zh", "x"))
    blocks, rows, orb = bcoef.shape[1:]
    points = zl * cores
    minor = points // SIDE
    core = lax.axis_index("c")
    high = lax.axis_index("zh")
    low = lax.axis_index("zl")
    here_y, here_x = lax.axis_index("y"), lax.axis_index("x")

    own_w = (here_y * zh + high) * xs + here_x
    own_k = low * cores + core
    target = kmq[0]
    major_shift = ((own_k >> 2) - (target >> 2)) & 3
    minor_shift = ((own_k & 3) - (target & 3)) & 3
    branch = (major_shift - 1) * (minor - 1) + minor_shift - 1

    swapped = [(c * zh + h, h * zh + c) for c in range(cores) for h in range(zh)]

    def partner(major, minor_by):
        route = []
        for k in range(points):
            a, b = divmod(k, minor)
            source = (a - major) % SIDE * minor + (b - minor_by) % minor
            for h in range(zh):
                route.append((source * zh + h, (k // cores * cores + h) * zh + k % cores))

        def work(shard, green_fwd, green_back):
            shard = shard.transpose(1, 0, 2).reshape(rows * blocks, orb)
            shard = lax.ppermute(shard, ("c", "zh"), swapped)
            green_fwd = lax.ppermute(green_fwd, ("c", "zh"), swapped)
            green_back = lax.ppermute(green_back, ("zl", "c", "zh"), route)
            mine = lax.cond(
                target >= 0,
                lambda block: spread(block, ("y", "x"), ys * xs),
                lambda block: jnp.zeros((ys * xs * block.shape[0], block.shape[1]), block.dtype),
                settled(shard),
            )
            return mine, green_fwd, green_back

        return work

    works = [partner(a, b) for a in range(1, SIDE) for b in range(1, minor)]
    mine, green_fwd, green_back = lax.switch(
        branch, works, bcoef[0], fwd_green[0, 0], back_green[0, 0]
    )
    mine, own_w, core = lax.optimization_barrier((mine, own_w.astype(jnp.uint32), core))
    other = lax.ppermute(mine, "c", [(0, 1), (1, 0)])
    coef_mine, left_mine, green_fwd, back_t = first_half(
        core[None], mine, green_fwd, green_back, blocks
    )
    pairs = product(coef_mine, left_mine, other, green_fwd, back_t, zl * zh, cores)
    pairs, ir_table, ir_fit, freq_index = lax.optimization_barrier(
        (pairs, ir_table, ir_fit, freq_index)
    )
    parts = lax.all_to_all(pairs, ("zl", "zh"), 0, 0, tiled=True)
    summed = jnp.sum(parts, axis=0)
    entries = jnp.broadcast_to(summed[:, None, :], (cores, ys * xs, blocks))
    entries = entries.reshape(cores * ys * xs, blocks)
    times = lax.all_to_all(entries, ("c", "y", "x"), 0, 0, tiled=True)
    chosen = lax.dynamic_slice_in_dim(ir_table, lax.dynamic_slice(freq_index, (own_w,), (1,))[0], 1, axis=1)
    fit = ir_fit.reshape(-1, ys, cores, xs).transpose(0, 2, 1, 3).reshape(ir_fit.shape)
    transform = jnp.sum(chosen.transpose(0, 2, 1) * fit[None], axis=1)
    result = jnp.sum(transform[:, :, None] * times[None], axis=1)
    return result[:, None, None, :]


def solution(mesh):
    sizes = {"zl": 8, "c": 2, "y": 4, "zh": 2, "x": 4}
    fine = Mesh(mesh.devices.reshape(tuple(sizes.values())), tuple(sizes))
    ka, tau = ("zl", "c"), ("y", "zh", "x")
    return jax.shard_map(
        functools.partial(shards, sizes),
        mesh=fine,
        in_specs=(
            P(ka, None, tau, None),
            P(ka, tau, None, None),
            P(ka, tau, None, None),
            P(ka),
            P(),
            P(),
            P(),
        ),
        out_specs=P(None, tau, ka, None),
        check_vma=False,
    )
```

```python
import functools

import jax
import jax.numpy as jnp
from jax import lax
from jax.experimental import pallas as pl
from jax.experimental.pallas import tpu as pltpu
from jax.sharding import Mesh
from jax.sharding import PartitionSpec as P

SIDE = 4
ROWS = 12
STEP = 4
TILE = 16
POINTS = 16
FIRST_LIMIT = 10 * 1024 * 1024
PRODUCT_LIMIT = 20 * 1024 * 1024
SMALL_LIMIT = 8 * 1024 * 1024
COST = pl.CostEstimate(flops=1000, bytes_accessed=1000, transcendentals=0)


def onehot(rows, columns):
    return (rows == columns).astype(jnp.float32).astype(jnp.bfloat16)


def swap_order(blocks):
    size = TILE * blocks
    at = lax.broadcasted_iota(jnp.int32, (size, size), 0)
    source = lax.broadcasted_iota(jnp.int32, (size, size), 1)
    return onehot(at % TILE * blocks + at // TILE, source)


def row_order(size, core):
    at = lax.broadcasted_iota(jnp.int32, (size, 1), 0)
    side = (at >= size // 2).astype(jnp.int32)
    here = core ^ side
    rest = at - side * (size // 2)
    shard = (rest * 171) >> 11
    row = rest - shard * ROWS
    y, x = shard >> 2, shard & 3
    return onehot(((y * 2 + here) * SIDE + x) * ROWS + row, lax.broadcasted_iota(jnp.int32, (size, size), 1))


def left_turn(order, piece_ref, fwd_ref, coef_ref, left_ref, turn, step):
    blocks = coef_ref.shape[0]
    width = fwd_ref.shape[-1]
    size = TILE * blocks
    pieces = [
        piece_ref[pl.ds(pl.multiple_of((turn * step + part) * size, size), size), :]
        for part in range(step)
    ]
    wide = jnp.dot(order, jnp.concatenate(pieces, axis=1), preferred_element_type=jnp.float32)
    wide = wide.astype(jnp.bfloat16)
    coefs = []
    for part in range(step):
        group = turn * step + part
        coef = wide[:, part * width : (part + 1) * width]
        spot = pl.ds(pl.multiple_of(group * TILE, TILE), TILE)
        coef_ref[:, spot, :] = coef.reshape(blocks, TILE, width)
        coefs.append(coef)
    left = jnp.dot(jnp.concatenate(coefs, axis=0), fwd_ref[...], preferred_element_type=jnp.float32)
    left = left.astype(jnp.bfloat16).reshape(step, blocks * TILE, width)
    for part in range(step):
        group = turn * step + part
        left_ref[:, pl.ds(pl.multiple_of(group * width, width), width)] = left[part]


def first_kernel(
    core_ref, piece_hbm, fwd_hbm, back_hbm, coef_ref, left_ref, fwd_ref, back_t_ref, piece_ref, back_ref, sems
):
    blocks = coef_ref.shape[0]
    order = swap_order(blocks)
    step = STEP
    turns = coef_ref.shape[1] // TILE // step
    size = step * TILE * blocks

    def piece_copy(turn):
        spot = pl.ds(pl.multiple_of(turn * size, size), size)
        return pltpu.make_async_copy(piece_hbm.at[spot], piece_ref.at[spot], sems.at[turn])

    fwd_copy = pltpu.make_async_copy(fwd_hbm, fwd_ref, sems.at[turns])
    back_copy = pltpu.make_async_copy(back_hbm, back_ref, sems.at[turns + 1])
    piece_copy(0).start()
    fwd_copy.start()
    for turn in range(1, turns):
        piece_copy(turn).start()
    back_copy.start()
    fwd_copy.wait()

    @pl.loop(0, turns)
    def _(turn):
        piece_copy(turn).wait()
        left_turn(order, piece_ref, fwd_ref, coef_ref, left_ref, turn, step)

    back_copy.wait()
    rows = row_order(back_ref.shape[0], core_ref[0])
    back = jnp.dot(rows, back_ref[...], preferred_element_type=jnp.float32).astype(jnp.bfloat16)
    back_t = lax.dot_general(
        rows, back, (((1,), (1,)), ((), ())), preferred_element_type=jnp.float32
    )
    back_t_ref[...] = back_t.astype(jnp.bfloat16)


def product_kernel(
    coef_mine_ref, left_mine_ref, piece_ref, fwd_ref, back_t_ref, out_ref, coef_other_ref, left_other_ref, right_ref
):
    blocks, half, width = coef_mine_ref.shape
    order = swap_order(blocks)

    @pl.loop(0, half // TILE // (STEP + 2))
    def _(turn):
        left_turn(order, piece_ref, fwd_ref, coef_other_ref, left_other_ref, turn, STEP + 2)

    per_side = half // TILE

    @pl.loop(0, blocks // 2, unroll=4)
    def _(pair):
        coefs = []
        for p in (2 * pair, 2 * pair + 1):
            coefs.append(jnp.concatenate([coef_mine_ref[p], coef_other_ref[p]], axis=0))
        right = jnp.dot(
            back_t_ref[...], jnp.concatenate(coefs, axis=1), preferred_element_type=jnp.float32
        )
        right = right.astype(jnp.bfloat16)
        for inner in range(2):
            rows = pl.ds(pl.multiple_of((2 * pair + inner) * TILE, TILE), TILE)
            for block in range(2 * per_side):
                at = block % per_side * width
                right_ref[block // per_side, rows, at : at + width] = right[
                    block * TILE : (block + 1) * TILE, inner * width : (inner + 1) * width
                ]

    size = TILE * blocks
    gram = jnp.zeros((size, size), jnp.float32)
    for side, lefts in enumerate((left_mine_ref, left_other_ref)):
        gram += lax.dot_general(
            lefts[...], right_ref[side], (((1,), (1,)), ((), ())), preferred_element_type=jnp.float32
        )
    row = lax.broadcasted_iota(jnp.int32, (size, size), 0) % TILE
    column = lax.broadcasted_iota(jnp.int32, (size, size), 1) % TILE
    gram = jnp.where(row == column, gram, 0.0)
    gram = jnp.sum(gram.reshape(blocks, TILE, size), axis=1)
    at = lax.broadcasted_iota(jnp.int32, (size, blocks), 0) // TILE
    which = lax.broadcasted_iota(jnp.int32, (size, blocks), 1)
    pick = (at == which).astype(jnp.float32)
    polar = jnp.dot(gram, pick, precision=lax.Precision.HIGHEST, preferred_element_type=jnp.float32)
    polar = polar * (-1.0 / POINTS)
    _, cores, _ = out_ref.shape
    for p in range(blocks):
        for copy in range(out_ref.shape[0] * cores // blocks):
            place = p // cores * (out_ref.shape[0] * cores // blocks) + copy
            out_ref[place, p % cores : p % cores + 1, :] = polar[p : p + 1, :]


def half_shapes(piece, blocks):
    width = piece.shape[-1]
    half = piece.shape[0] // blocks
    coef = jax.ShapeDtypeStruct((blocks, half, width), jnp.bfloat16)
    left = jax.ShapeDtypeStruct((blocks * TILE, half // TILE * width), jnp.bfloat16)
    return coef, left


def first_half(core, piece, green_fwd, green_back, blocks):
    width = green_fwd.shape[-1]
    square = jax.ShapeDtypeStruct((width, width), jnp.bfloat16)
    return pl.pallas_call(
        first_kernel,
        out_shape=half_shapes(piece, blocks) + (square, square),
        in_specs=[pl.BlockSpec(memory_space=pltpu.SMEM)]
        + [pl.BlockSpec(memory_space=pl.ANY)] * 3,
        out_specs=[pl.BlockSpec(memory_space=pltpu.VMEM)] * 4,
        scratch_shapes=[
            pltpu.VMEM(piece.shape, jnp.bfloat16),
            pltpu.VMEM((width, width), jnp.bfloat16),
            pltpu.SemaphoreType.DMA((piece.shape[0] // (STEP * TILE * blocks) + 2,)),
        ],
        compiler_params=pltpu.CompilerParams(vmem_limit_bytes=FIRST_LIMIT),
        cost_estimate=COST,
    )(core, piece, green_fwd, green_back)


def product(coef_mine, left_mine, other, green_fwd, back_t, receivers, cores):
    blocks, half, width = coef_mine.shape
    return pl.pallas_call(
        product_kernel,
        out_shape=jax.ShapeDtypeStruct((receivers, cores, blocks), jnp.float32),
        in_specs=[pl.BlockSpec(memory_space=pltpu.VMEM)] * 5,
        out_specs=pl.BlockSpec(memory_space=pltpu.VMEM),
        scratch_shapes=[
            pltpu.VMEM(coef_mine.shape, jnp.bfloat16),
            pltpu.VMEM(left_mine.shape, jnp.bfloat16),
            pltpu.VMEM((2, blocks * TILE, half // TILE * width), jnp.bfloat16),
        ],
        compiler_params=pltpu.CompilerParams(vmem_limit_bytes=PRODUCT_LIMIT),
        cost_estimate=COST,
    )(coef_mine, left_mine, other, green_fwd, back_t)


def settle_kernel(block_ref, out_ref):
    out_ref[...] = block_ref[...]


def settled(block):
    return pl.pallas_call(
        settle_kernel,
        out_shape=jax.ShapeDtypeStruct(block.shape, block.dtype),
        in_specs=[pl.BlockSpec(memory_space=pltpu.VMEM)],
        out_specs=pl.BlockSpec(memory_space=pltpu.VMEM),
        compiler_params=pltpu.CompilerParams(vmem_limit_bytes=SMALL_LIMIT),
        cost_estimate=pl.CostEstimate(
            flops=50_000_000_000, bytes_accessed=2_500_000, transcendentals=0
        ),
    )(block)


def spread(block, axes, count):
    copies = jnp.broadcast_to(block[None], (count,) + block.shape)
    rows = lax.all_to_all(copies, axes, 0, 0, tiled=True)
    return rows.reshape(count * block.shape[0], block.shape[1])


def shards(sizes, bcoef, fwd_green, back_green, kmq, ir_table, ir_fit, freq_index):
    zl, cores, ys, zh, xs = (sizes[name] for name in ("zl", "c", "y", "zh", "x"))
    blocks, rows, orb = bcoef.shape[1:]
    points = zl * cores
    minor = points // SIDE
    core = lax.axis_index("c")
    high = lax.axis_index("zh")
    low = lax.axis_index("zl")
    here_y, here_x = lax.axis_index("y"), lax.axis_index("x")

    own_w = (here_y * zh + high) * xs + here_x
    own_k = low * cores + core
    target = kmq[0]
    major_shift = ((own_k >> 2) - (target >> 2)) & 3
    minor_shift = ((own_k & 3) - (target & 3)) & 3
    branch = (major_shift - 1) * (minor - 1) + minor_shift - 1

    swapped = [(c * zh + h, h * zh + c) for c in range(cores) for h in range(zh)]

    def partner(major, minor_by):
        route = []
        for k in range(points):
            a, b = divmod(k, minor)
            source = (a - major) % SIDE * minor + (b - minor_by) % minor
            for h in range(zh):
                route.append((source * zh + h, (k // cores * cores + h) * zh + k % cores))

        def work(shard, green_fwd, green_back):
            shard = shard.transpose(1, 0, 2).reshape(rows * blocks, orb)
            shard = lax.ppermute(shard, ("c", "zh"), swapped)
            green_fwd = lax.ppermute(green_fwd, ("c", "zh"), swapped)
            green_back = lax.ppermute(green_back, ("zl", "c", "zh"), route)
            mine = lax.cond(
                target >= 0,
                lambda block: spread(block, ("y", "x"), ys * xs),
                lambda block: jnp.zeros((ys * xs * block.shape[0], block.shape[1]), block.dtype),
                settled(shard),
            )
            return mine, green_fwd, green_back

        return work

    works = [partner(a, b) for a in range(1, SIDE) for b in range(1, minor)]
    mine, green_fwd, green_back = lax.switch(
        branch, works, bcoef[0], fwd_green[0, 0], back_green[0, 0]
    )
    mine, own_w, core = lax.optimization_barrier((mine, own_w.astype(jnp.uint32), core))
    other = lax.ppermute(mine, "c", [(0, 1), (1, 0)])
    coef_mine, left_mine, green_fwd, back_t = first_half(
        core[None], mine, green_fwd, green_back, blocks
    )
    pairs = product(coef_mine, left_mine, other, green_fwd, back_t, zl * zh, cores)
    pairs, ir_table, ir_fit, freq_index = lax.optimization_barrier(
        (pairs, ir_table, ir_fit, freq_index)
    )
    parts = lax.all_to_all(pairs, ("zl", "zh"), 0, 0, tiled=True)
    summed = jnp.sum(parts, axis=0)
    entries = jnp.broadcast_to(summed[:, None, :], (cores, ys * xs, blocks))
    entries = entries.reshape(cores * ys * xs, blocks)
    times = lax.all_to_all(entries, ("c", "y", "x"), 0, 0, tiled=True)
    chosen = lax.dynamic_slice_in_dim(ir_table, lax.dynamic_slice(freq_index, (own_w,), (1,))[0], 1, axis=1)
    fit = ir_fit.reshape(-1, ys, cores, xs).transpose(0, 2, 1, 3).reshape(ir_fit.shape)
    transform = jnp.sum(chosen.transpose(0, 2, 1) * fit[None], axis=1)
    result = jnp.sum(transform[:, :, None] * times[None], axis=1)
    return result[:, None, None, :]


def solution(mesh):
    sizes = {"zl": 8, "c": 2, "y": 4, "zh": 2, "x": 4}
    fine = Mesh(mesh.devices.reshape(tuple(sizes.values())), tuple(sizes))
    ka, tau = ("zl", "c"), ("y", "zh", "x")
    return jax.shard_map(
        functools.partial(shards, sizes),
        mesh=fine,
        in_specs=(
            P(ka, None, tau, None),
            P(ka, tau, None, None),
            P(ka, tau, None, None),
            P(ka),
            P(),
            P(),
            P(),
        ),
        out_specs=P(None, tau, ka, None),
        check_vma=False,
    )
```
